32 devices in a mesh: slab: 4 (over z), dom: 8 (over y, x, core).
Axes of the slice: x: 2, y: 2, z: 4, core: 2. Of those that a mesh axis runs over, the one named last changes fastest.
Arguments:
- initial_field: float32 [105, 163840], P(None, ('slab', 'dom')), may hold values from -6 to 6
- cotangent: float32 [105, 163840], P(None, ('slab', 'dom')), may hold values from -6 to 6
- jacobian: float32 [163840], P(('slab', 'dom')), may hold values from 0.5 to 2
- conductivity: float32 [163840], P(('slab', 'dom')), may hold values from 0.3 to 3
- block_level: int32 [640], P(('slab', 'dom')), may hold values from 0 to 2, as said below
- face_link: int32 [4, 163840], P(None, ('slab', 'dom')), may hold values from 0 to 36863, as said below
- stiff: bfloat16 [105, 105], replicated, may hold values from -0.625 to 0.625
- lift: bfloat16 [105, 180], replicated, may hold values from -0.4375 to 0.4375
- trace_op: bfloat16 [180, 105], replicated, may hold values from -0.625 to 0.625
Outputs:
- adjoint_field: float32 [105, 163840], P(None, ('slab', 'dom'))
- conductivity_grad: float32 [163840], P(('slab', 'dom'))
The draws below stay inside these ranges and needn't reach their ends.
Inputs may be any that keep to these rules, and one draw needn't show every extreme that they name: `block_level`: within each partition's 20 consecutive blocks the level never rises, and the first block has level 2. `face_link`: A code 4 n + k names face k of buffer column n; columns 5120 and beyond are named only by the first 1024 elements of a partition, and face j only names the j-th received region.
All inputs are finite; a program needn't handle non-finite values.
Results may differ from the reference program's by a relative error of at most 0.0015.
Values may be sent and summed in bfloat16 or wider, within the bound.
No kernel may reach another device: no remote copies, remote signals or barrier semaphores. Data moves between devices by JAX's collectives and lax.ppermute only.
A program may use at most 192 MiB of HBM per device.

```python
import math
import jax
import jax.numpy as jnp
from jax import lax

W = 105
FW = 180
BLK = 256
NBLK = 20
BOUND = 1024
NBLKS = 640
ELEMS = 163840
N_SLAB = 4
N_DOM = 8


def draw_block_level(key, part):
    count = NBLKS // NBLK
    keys = jax.random.split(jax.random.fold_in(key, 7), 5)
    busy = jax.random.randint(keys[0], (count,), 0, 8) == 0
    chosen = jax.random.randint(keys[1], (), 0, count)
    busy = busy | (jnp.arange(count) == chosen)
    heavy = jax.random.randint(keys[2], (count,), NBLK // 2, NBLK + 1)
    light = jax.random.randint(keys[3], (count,), 1, NBLK // 8 + 1)
    finest = jnp.where(busy, heavy, light)
    middle = jnp.minimum(jax.random.randint(keys[4], (count,), 0, NBLK + 1), NBLK - finest)
    position = jnp.arange(NBLK)[None, :]
    level = jnp.where(position < finest[:, None], 2, jnp.where(position < (finest + middle)[:, None], 1, 0))
    return level.reshape(-1).astype(jnp.int32)


def draw_face_link(key, part):
    per_dev = NBLK * BLK
    total = NBLKS * BLK
    keys = jax.random.split(jax.random.fold_in(key, 13), 4)
    local_pos = jnp.arange(total) % per_dev
    near = local_pos < BOUND
    remote = (jax.random.randint(keys[0], (4, total), 0, 2) == 1) & near[None, :]
    region = jnp.arange(4)[:, None]
    far_slot = per_dev + region * BOUND + jax.random.randint(keys[1], (4, total), 0, BOUND)
    near_slot = jax.random.randint(keys[2], (4, total), 0, per_dev)
    target = jnp.where(remote, far_slot, near_slot)
    face_num = jax.random.randint(keys[3], (4, total), 0, 4)
    return (4 * target + face_num).astype(jnp.int32)


def block_levels(key, dims, cuts, smallest, largest):
    loudness = 1.0
    for dim, shards_of in cuts:
        steps = jax.random.uniform(jax.random.fold_in(jax.random.fold_in(key, 6), dim), (shards_of,), jnp.float32, smallest / len(cuts), largest / len(cuts))
        loudness = loudness * jnp.repeat(jnp.exp(steps), dims[dim] // shards_of).reshape((-1,) + (1,) * (len(dims) - 1 - dim))
    return loudness


def gaussian(own_key, shape, deviation, bound, cuts=(), held_as=jnp.bfloat16):
    values = jax.random.normal(own_key, shape, jnp.float32) * deviation
    if len(cuts) > 0:
        values = block_levels(own_key, shape, cuts, -0.22, 0.18) * values
    return jnp.clip(values, min=-bound, max=bound).astype(held_as)


def setup_inputs(seed: int = 0) -> dict:
    arg_keys = jax.random.split(jax.random.key(seed), 10)
    initial_field = gaussian(arg_keys[0], (W, ELEMS), 1.0, 6.0, ((1, 32),), jnp.float32)
    cotangent = gaussian(arg_keys[1], (W, ELEMS), 1.0, 6.0, ((1, 32),), jnp.float32)
    jacobian = jnp.clip(jnp.exp(math.log(2.0) - 1.3862944 * jax.random.uniform(arg_keys[2], (ELEMS,), jnp.float32) ** block_levels(arg_keys[2], (ELEMS,), ((0, 32),), -0.2, 0.2)), 0.5, 2.0)
    conductivity = jnp.clip(jnp.exp(math.log(3.0) - 2.3025851 * jax.random.uniform(arg_keys[3], (ELEMS,), jnp.float32) ** block_levels(arg_keys[3], (ELEMS,), ((0, 32),), -0.2, 0.2)), 0.3, 3.0)
    block_level = draw_block_level(jax.random.fold_in(arg_keys[9], 71), 0)
    face_link = draw_face_link(jax.random.fold_in(arg_keys[9], 71), 0)
    stiff = gaussian(arg_keys[6], (W, W), W ** -0.5, 0.625)
    lift = gaussian(arg_keys[7], (W, FW), FW ** -0.5, 0.4375)
    trace_op = gaussian(arg_keys[8], (FW, W), W ** -0.5, 0.625)
    return {"initial_field": initial_field, "cotangent": cotangent, "jacobian": jacobian, "conductivity": conductivity, "block_level": block_level, "face_link": face_link, "stiff": stiff, "lift": lift, "trace_op": trace_op}


base_step = 0.05
lowest_level = (2, 1, 2, 0)


def step_sizes(levels, substep):
    size_one = jnp.where(levels == 2, base_step, jnp.where(levels == 1, 2.0 * base_step, 4.0 * base_step))
    return jnp.where(levels >= lowest_level[substep], size_one, 0.0).astype(jnp.float32)


def link_columns(link_codes, buffer_len):
    return ((link_codes % 4) * buffer_len + link_codes // 4).reshape(-1)


def reference(initial_field, cotangent, jacobian, conductivity, block_level, face_link, stiff, lift, trace_op):
    devices = N_SLAB * N_DOM
    elements = NBLK * BLK
    nodes_face = FW // 4
    buffer_len = elements + 4 * BOUND
    trace_wide = trace_op.astype(jnp.float32)

    def split_rows(array):
        return array.reshape(array.shape[0], devices, elements).transpose(1, 0, 2)

    def join_rows(array):
        return array.transpose(1, 0, 2).reshape(array.shape[1], devices * elements)

    state_zero = split_rows(initial_field)
    adjoint = split_rows(cotangent)
    jac_dev = jacobian.reshape(devices, elements)
    cond_dev = conductivity.reshape(devices, elements)
    links = split_rows(face_link)
    levels = jnp.repeat(block_level.reshape(devices, NBLK), BLK, axis=1)

    def neighbours(edge):
        grid = edge.reshape(N_SLAB, N_DOM, FW, BOUND)
        zero_slab = jnp.zeros_like(grid[:1])
        zero_dom = jnp.zeros_like(grid[:, :1])
        lower_slab = jnp.concatenate([zero_slab, grid[:-1]], axis=0)
        upper_slab = jnp.concatenate([grid[1:], zero_slab], axis=0)
        lower_dom = jnp.concatenate([zero_dom, grid[:, :-1]], axis=1)
        upper_dom = jnp.concatenate([grid[:, 1:], zero_dom], axis=1)
        joined = jnp.concatenate([lower_slab, upper_slab, lower_dom, upper_dom], axis=3)
        return joined.reshape(devices, FW, 4 * BOUND)

    def returned(extra):
        row_count = extra.shape[1]
        grid = extra.reshape(N_SLAB, N_DOM, row_count, 4, BOUND)
        zero_slab = jnp.zeros_like(grid[:1, :, :, 0])
        zero_dom = jnp.zeros_like(grid[:, :1, :, 0])
        total = jnp.concatenate([grid[1:, :, :, 0], zero_slab], axis=0)
        total = total + jnp.concatenate([zero_slab, grid[:-1, :, :, 1]], axis=0)
        total = total + jnp.concatenate([grid[:, 1:, :, 2], zero_dom], axis=1)
        total = total + jnp.concatenate([zero_dom, grid[:, :-1, :, 3]], axis=1)
        return total.reshape(devices, row_count, BOUND)

    def trace_device(state_now):
        return jnp.dot(trace_op, state_now.astype(jnp.bfloat16), preferred_element_type=jnp.float32).astype(jnp.bfloat16)

    def advance(states, substep):
        traces = lax.map(trace_device, states)
        arrived = neighbours(traces[:, :, :BOUND])
        step_len = step_sizes(levels, substep)

        def one_device(pieces):
            state_now, trace_now, arrived_now, link_codes, jac_now, cond_now, step_now = pieces
            flat_buffer = jnp.concatenate([trace_now, arrived_now], axis=1).reshape(nodes_face, 4 * buffer_len)
            gathered = jnp.take(flat_buffer, link_columns(link_codes, buffer_len), axis=1).reshape(nodes_face, 4, elements)
            own_part = trace_now.reshape(nodes_face, 4, elements)
            jump_low = (gathered.astype(jnp.float32) - own_part.astype(jnp.float32)).astype(jnp.bfloat16).reshape(FW, elements)
            state_low = state_now.astype(jnp.bfloat16)
            change = jac_now * (jnp.dot(stiff, state_low, preferred_element_type=jnp.float32)
                                + jnp.dot(lift, jump_low, preferred_element_type=jnp.float32)) - cond_now * state_now
            return state_now + step_now * change

        return lax.map(one_device, (states, traces, arrived, links, jac_dev, cond_dev, step_len))

    def retreat(adjoint_now, states, substep):
        step_len = step_sizes(levels, substep)
        scaled = step_len[:, None, :] * adjoint_now
        grad_part = -jnp.sum(scaled * states, axis=1)

        def spread_device(pieces):
            scaled_now, link_codes, jac_now = pieces
            weighted_low = (jac_now * scaled_now).astype(jnp.bfloat16)
            lifted = jnp.dot(lift.T, weighted_low, preferred_element_type=jnp.float32)
            scatter_acc = jnp.zeros((nodes_face, 4 * buffer_len), jnp.float32)
            scatter_acc = scatter_acc.at[:, link_columns(link_codes, buffer_len)].add(lifted.reshape(nodes_face, 4 * elements))
            scattered = scatter_acc.reshape(FW, buffer_len)
            stiff_part = jnp.dot(stiff.T, weighted_low, preferred_element_type=jnp.float32)
            projected = jnp.dot(trace_wide.T, scattered[:, elements:], precision=lax.Precision.HIGHEST)
            return scattered[:, :elements] - lifted, projected, stiff_part

        own_part, extra, stiff_part = lax.map(spread_device, (scaled, links, jac_dev))
        incoming = returned(extra)

        def finish_device(pieces):
            own_now, incoming_now, stiff_now, adjoint_here, scaled_now, cond_now = pieces
            back_part = stiff_now + jnp.dot(trace_op.T, own_now.astype(jnp.bfloat16), preferred_element_type=jnp.float32)
            back_part = back_part.at[:, :BOUND].add(incoming_now)
            return adjoint_here - cond_now * scaled_now + back_part

        updated = lax.map(finish_device, (own_part, incoming, stiff_part, adjoint_now, scaled, cond_dev))
        return updated, grad_part

    saved = [state_zero]
    for substep in range(3):
        saved.append(advance(saved[-1], substep))
    gradient = jnp.zeros((devices, elements), jnp.float32)
    for substep in (3, 2, 1, 0):
        adjoint, grad_part = retreat(adjoint, saved[substep], substep)
        gradient = gradient + grad_part
    return join_rows(adjoint), gradient.reshape(-1)
```

```python
import functools

import jax
import jax.numpy as jnp
from jax import lax
from jax.experimental import pallas as pl
from jax.experimental.pallas import tpu as pltpu
from jax.sharding import PartitionSpec as P

BLK = 256
BOUND = 1024
BB = BOUND // BLK
LANES = 128
HALF = 64
UNROLL = 128
SPREAD = 64
F32 = jnp.float32
BF16 = jnp.bfloat16

base_step = 0.05
lowest_level = (2, 1, 2, 0)

SMEM = pl.BlockSpec(memory_space=pltpu.SMEM)
VMEM = pl.BlockSpec(memory_space=pltpu.VMEM)
ANY = pl.BlockSpec(memory_space=pl.ANY)


def mm(a, b):
    return jnp.dot(a, b, preferred_element_type=F32)


def block_step(level):
    return jnp.where(
        level == 2, base_step, jnp.where(level == 1, 2.0 * base_step, 4.0 * base_step)
    ).astype(F32)


def active_blocks(level_ref, blocks, lowest):
    count = jnp.int32(0)
    for b in range(blocks):
        count = count + jnp.where(level_ref[b] >= lowest, 1, 0)
    return count


def rows_of(b):
    return pl.ds(pl.multiple_of(b * BLK, BLK), BLK)


def move_rows(idx_ref, flag_ref, block, source, accs, p_ref, g_ref):
    groups = 4 * BLK // UNROLL

    def group(q, _):
        base = pl.multiple_of(block * (4 * BLK) + q * UNROLL, UNROLL)
        pos = pl.multiple_of(q * UNROLL, UNROLL)

        def fast():
            for t in range(UNROLL // 4):
                acc = accs[t % 2]
                ii = [idx_ref[base + 4 * t + r] for r in range(4)]
                vals = [acc[pl.ds(i, 1), :] for i in ii]
                if g_ref is not None:
                    for r in range(4):
                        got = vals[r] if source is None else source[pl.ds(ii[r], 1), :]
                        g_ref[pl.ds(pos + 4 * t + r, 1), :] = got
                for r in range(4):
                    acc[pl.ds(ii[r], 1), :] = vals[r] + p_ref[pl.ds(pos + 4 * t + r, 1), :]

        def slow():
            acc = accs[0]

            def one(r, _):
                i = idx_ref[base + r]
                val = acc[pl.ds(i, 1), :]
                if g_ref is not None:
                    g_ref[pl.ds(pos + r, 1), :] = val if source is None else source[pl.ds(i, 1), :]
                acc[pl.ds(i, 1), :] = val + p_ref[pl.ds(pos + r, 1), :]
                return 0

            lax.fori_loop(0, UNROLL, one, 0)

        clash = flag_ref[block * groups + q]
        pl.when(clash == 0)(fast)
        pl.when(clash != 0)(slow)
        return 0

    lax.fori_loop(0, groups, group, 0)


def prep_kernel(x_ref, c_ref, s_ref, u_out, lam_out, geo_out, buf):
    width = x_ref.shape[0]
    buf[...] = jnp.zeros_like(buf)
    buf[:width, :] = x_ref[...]
    u_out[...] = buf[...].T
    buf[:width, :] = c_ref[...]
    lam_out[...] = buf[...].T
    buf[...] = jnp.zeros_like(buf)
    buf[: s_ref.shape[0], :] = s_ref[...]
    geo_out[...] = buf[...].T


def boundary_kernel(lowest, fwd, first, elements, *refs):
    refs = list(refs)
    idx_ref, flag_ref, level_ref, geo_hbm, u_ref, lam_hbm = refs[:6]
    del refs[:6]
    arrived = []
    if not first:
        arrived = refs[:4]
        del refs[:4]
    lift_back, trace_back, trace_fwd, lift_fwd = refs[:4]
    del refs[:4]
    lam_hbm_out, u_out = refs[:2]
    sends = refs[2:6]
    ubuf, acc0, acc1, p_ref, g_ref, geo_ref, lam_ref, sems = refs[6:]
    blocks = level_ref.shape[0]
    active = jnp.minimum(active_blocks(level_ref, blocks, lowest), BB)
    edge = pl.ds(0, BOUND)
    loads = [
        pltpu.make_async_copy(geo_hbm.at[edge], geo_ref, sems.at[0]),
        pltpu.make_async_copy(lam_hbm.at[edge], lam_ref, sems.at[1]),
        pltpu.make_async_copy(
            u_ref if fwd else u_ref.at[edge], ubuf.at[pl.ds(0, u_ref.shape[0] if fwd else BOUND)], sems.at[2]
        ),
    ]
    for copy in loads:
        copy.start()

    def zero(b, _):
        at = pl.ds(pl.multiple_of(elements + b * BLK, BLK), BLK)
        acc0[at, :] = jnp.zeros((BLK, LANES), F32)
        acc1[at, :] = jnp.zeros((BLK, LANES), F32)
        return 0

    if fwd:
        for r in range(4):
            ubuf[elements + r * BOUND : elements + (r + 1) * BOUND, :] = arrived[r][0].astype(F32)
    lax.fori_loop(0, 4 * BB, zero, 0)
    for copy in loads:
        copy.wait()

    def full_lam(b):
        lam = lam_ref[rows_of(b), :]
        for a in arrived:
            lam = lam + a[1, rows_of(b), :].astype(F32)
        lam_ref[rows_of(b), :] = lam
        return lam

    group = lax.broadcasted_iota(jnp.int32, (BLK, 4 * HALF), 1) // HALF
    group = group.astype(F32)

    def busy(b, _):
        lam = full_lam(b)
        geo = geo_ref[rows_of(b), :]
        jac, cond = geo[:, 0:1], geo[:, 1:2]
        step = block_step(level_ref[b])
        weighted = (jac * (step * lam)).astype(BF16)
        masks = [group == geo[:, 2 + j : 3 + j] for j in range(4)]
        for j in range(4):
            lifted = mm(weighted, lift_back[j])
            lifted = jnp.where(masks[j], lifted, 0.0).astype(BF16)
            p_ref[j * BLK : (j + 1) * BLK, :] = mm(lifted, trace_back[...])
        move_rows(
            idx_ref, flag_ref, b, ubuf, (acc0, acc1), p_ref, g_ref if fwd else None
        )
        u = ubuf[rows_of(b), :]
        if fwd:
            low = u.astype(BF16)
            change = mm(jnp.concatenate([low, low], axis=1), lift_fwd[4 * 4 * HALF :, :])
            for j in range(4):
                traces = mm(g_ref[j * BLK : (j + 1) * BLK, :].astype(BF16), trace_fwd[...])
                traces = jnp.where(masks[j], traces, 0.0).astype(BF16)
                change = change + mm(traces, lift_fwd[j * 4 * HALF : (j + 1) * 4 * HALF, :])
            u = u + step * (jac * change - cond * u)
        u_out[rows_of(b), :] = u
        return 0

    def idle(b, _):
        full_lam(b)
        u_out[rows_of(b), :] = ubuf[rows_of(b), :]
        return 0

    lax.fori_loop(0, active, busy, 0)
    lax.fori_loop(active, BB, idle, 0)
    store = pltpu.make_async_copy(lam_ref, lam_hbm_out.at[edge], sems.at[3])
    store.start()

    for send, region in zip(sends, (1, 0, 3, 2), strict=True):
        at = slice(elements + region * BOUND, elements + (region + 1) * BOUND)
        send[0] = u_out[...].astype(BF16)
        send[1] = (acc0[at, :] + acc1[at, :]).astype(BF16)
    store.wait()


def interior_kernel(lowest, fwd, elements, *refs):
    refs = list(refs)
    idx_ref, flag_ref, level_ref, geo_ref, lam_ref = refs[:5]
    del refs[:5]
    if fwd:
        u_ref, edge_ref = refs[:2]
        del refs[:2]
    lift_back, own_back, trace_back, trace_fwd, all_fwd = refs[:5]
    del refs[:5]
    lam_out = refs.pop(0)
    if fwd:
        u_out = refs.pop(0)
    tab0, tab1, p_ref, g_ref = refs
    blocks = level_ref.shape[0]
    active = active_blocks(level_ref, blocks, lowest)

    def plane(b, k):
        return pl.ds(pl.multiple_of(k * elements + b * BLK, BLK), BLK)

    def start(b, _):
        if fwd:
            traces = mm(u_ref[rows_of(b), :].astype(BF16), trace_fwd[...])
            traces = traces.astype(BF16).astype(F32)
        else:
            traces = jnp.zeros((BLK, 4 * LANES), F32)
        for k in range(4):
            part = traces[:, k * LANES : (k + 1) * LANES]
            tab0[plane(b, k), :] = part
            tab1[plane(b, k), :] = part
        return 0

    lax.fori_loop(0, blocks, start, 0)

    def busy(b, _):
        lam = lam_ref[rows_of(b), :]
        geo = geo_ref[rows_of(b), :]
        jac, cond = geo[:, 0:1], geo[:, 1:2]
        step = block_step(level_ref[b])
        scaled = step * lam
        weighted = (jac * scaled).astype(BF16)
        lifted = mm(weighted, lift_back[...])
        for j in range(4):
            p_ref[j * BLK : (j + 1) * BLK, :] = lifted[:, j * LANES : (j + 1) * LANES]
        own = mm(jnp.concatenate([weighted, weighted], axis=1), own_back[...])
        lam_out[rows_of(b), :] = lam - cond * scaled + own
        if not fwd:
            move_rows(idx_ref, flag_ref, b, None, (tab0, tab1), p_ref, None)
            return 0

        @pl.when(b < BB)
        def _():
            move_rows(idx_ref, flag_ref, b, None, (tab0, tab1), p_ref, None)
            u_out[rows_of(b), :] = edge_ref[rows_of(b), :]

        @pl.when(b >= BB)
        def _():
            move_rows(idx_ref, flag_ref, b, None, (tab0, tab1), p_ref, g_ref)
            u = u_ref[rows_of(b), :]
            low = u.astype(BF16)
            parts = [g_ref[j * BLK : (j + 1) * BLK, :].astype(BF16) for j in range(4)]
            change = mm(jnp.concatenate(parts + [low, low], axis=1), all_fwd[...])
            u_out[rows_of(b), :] = u + step * (jac * change - cond * u)

        return 0

    def idle(b, _):
        lam_out[rows_of(b), :] = lam_ref[rows_of(b), :]
        if fwd:
            u_out[rows_of(b), :] = u_ref[rows_of(b), :]
        return 0

    lax.fori_loop(0, active, busy, 0)
    lax.fori_loop(active, blocks, idle, 0)

    def collect(b, _):
        parts = [
            (tab0[plane(b, k), :] + tab1[plane(b, k), :]).astype(BF16) for k in range(4)
        ]
        back = mm(jnp.concatenate(parts, axis=1), trace_back[...])
        lam_out[rows_of(b), :] = lam_out[rows_of(b), :] + back
        return 0

    lax.fori_loop(0, blocks, collect, 0)


def final_kernel(level_ref, *refs):
    arrived = refs[:4]
    lams = refs[4:9]
    states = refs[9:13]
    adj_out, grad_out, buf = refs[13:]
    b = pl.program_id(0)
    buf[...] = lams[0][...]

    @pl.when(b < BB)
    def _():
        total = lams[0][...]
        for a in arrived:
            total = total + a[0].astype(F32)
        buf[...] = total

    adj_out[...] = buf[...].T[: adj_out.shape[0], :]
    level = level_ref[b]
    total = jnp.zeros((BLK, LANES), F32)
    for s in range(4):
        step = jnp.where(level >= lowest_level[s], block_step(level), 0.0)
        total = total + (step * lams[s + 1][...]) * states[s][...]
    grad_out[...] = -jnp.sum(total.T, axis=0, keepdims=True)


def clash_flags(idx):
    q = idx.reshape(-1, 4)
    bad = jnp.zeros((q.shape[0],), jnp.bool_)
    for i in range(4):
        for j in range(i):
            bad = bad | (q[:, i] == q[:, j])
    return jnp.any(bad.reshape(-1, UNROLL // 4), axis=1).astype(jnp.int32)


def exchange(parts):
    out = []
    for part, axis, up in zip(
        parts, ("slab", "slab", "dom", "dom"), (True, False, True, False), strict=True
    ):
        pairs = [(i, i + 1) for i in range(lax.axis_size(axis) - 1)]
        if not up:
            pairs = [(j, i) for i, j in pairs]
        out.append(lax.ppermute(part, axis, pairs))
    return out


def local(
    initial_field, cotangent, jacobian, conductivity, block_level, face_link, stiff, lift, trace_op
):
    width, elements = initial_field.shape
    face_rows = trace_op.shape[0]
    nodes = face_rows // 4
    blocks = elements // BLK

    slot, face = face_link // 4, face_link % 4
    position = lax.broadcasted_iota(jnp.int32, face_link.shape, 1)
    own_row = jnp.where(
        slot < elements, face * elements + slot, 4 * elements + position % SPREAD
    )

    def by_block(a):
        count = a.shape[1] // BLK
        return a.reshape(4, count, BLK).transpose(1, 0, 2).reshape(-1)

    idx_in = by_block(own_row)
    idx_edge = by_block(slot[:, :BOUND])
    flag_in = clash_flags(idx_in)
    flag_edge = clash_flags(idx_edge)
    small = jnp.concatenate(
        [jacobian[None], conductivity[None], face.astype(F32), jnp.zeros((2, elements), F32)], axis=0
    )

    pad_w = LANES - width
    trace3 = trace_op.reshape(nodes, 4, width)
    lift3 = lift.reshape(width, nodes, 4)
    tail = LANES - nodes
    trace_fwd = jnp.pad(trace3.transpose(2, 1, 0), ((0, pad_w), (0, 0), (0, tail))).reshape(LANES, 4 * LANES)
    trace_back = jnp.pad(
        trace3.transpose(1, 0, 2), ((0, 0), (HALF, HALF - nodes), (0, pad_w))
    ).reshape(4 * LANES, LANES)
    lift_back = jnp.pad(
        lift3.transpose(0, 2, 1), ((0, pad_w), (0, 0), (HALF, HALF - nodes))
    ).reshape(LANES, 4 * LANES)
    lift_fwd = jnp.pad(lift3.transpose(2, 1, 0), ((0, 0), (0, tail), (0, pad_w))).reshape(4 * LANES, LANES)
    own = stiff.astype(F32) - mm(lift, trace_op)
    high = lax.reduce_precision(own, 8, 7)
    pair = jnp.stack([high, own - high]).astype(BF16)
    own_back = jnp.pad(pair, ((0, 0), (0, pad_w), (0, pad_w))).reshape(2 * LANES, LANES)
    own_fwd = jnp.pad(pair.transpose(0, 2, 1), ((0, 0), (0, pad_w), (0, pad_w))).reshape(2 * LANES, LANES)
    all_fwd = jnp.concatenate([lift_fwd, own_fwd], axis=0)
    edge_trace_fwd = trace_fwd.reshape(LANES, 4, LANES)[:, :, :HALF].reshape(LANES, 4 * HALF)
    edge_trace_back = trace_back.reshape(4, LANES, LANES)[:, HALF:].reshape(4 * HALF, LANES)
    edge_lift_back = jnp.tile(
        lift_back.reshape(LANES, 4, LANES)[:, :, HALF:].transpose(1, 0, 2), (1, 1, 4)
    )
    edge_lift_fwd = jnp.tile(lift_fwd.reshape(4, LANES, LANES)[:, :HALF], (1, 4, 1)).reshape(16 * HALF, LANES)
    edge_all_fwd = jnp.concatenate([edge_lift_fwd, own_fwd], axis=0)

    row = jax.ShapeDtypeStruct((elements, LANES), F32)
    edge_row = jax.ShapeDtypeStruct((BOUND, LANES), F32)
    payload = jax.ShapeDtypeStruct((2, BOUND, LANES), BF16)
    column = pl.BlockSpec((width, BLK), lambda b: (0, b))
    block = pl.BlockSpec((BLK, LANES), lambda b: (b, 0))

    state, lam, geo = pl.pallas_call(
        prep_kernel,
        grid=(blocks,),
        out_shape=(row, row, row),
        in_specs=[column, column, pl.BlockSpec((8, BLK), lambda b: (0, b))],
        out_specs=(block, block, block),
        scratch_shapes=[pltpu.VMEM((LANES, BLK), F32)],
        name="prep",
    )(initial_field, cotangent, small)

    buffer_len = elements + 4 * BOUND
    arrived = None
    states = [state]
    lams = []
    for stage in range(4):
        fwd = stage > 0
        lowest = lowest_level[3 - stage]
        args = [idx_edge, flag_edge, block_level, geo, state, lam]
        specs = [SMEM, SMEM, SMEM, ANY, ANY, ANY]
        if fwd:
            args += arrived
            specs += [VMEM] * 4
        args += [edge_lift_back, edge_trace_back, edge_trace_fwd, edge_all_fwd]
        specs += [VMEM] * 4
        outs = pl.pallas_call(
            functools.partial(boundary_kernel, lowest, fwd, not fwd, elements),
            out_shape=(row, edge_row) + (payload,) * 4,
            in_specs=specs,
            out_specs=(ANY, VMEM) + (VMEM,) * 4,
            scratch_shapes=[
                pltpu.VMEM((buffer_len, LANES), F32),
                pltpu.VMEM((buffer_len, LANES), F32),
                pltpu.VMEM((buffer_len, LANES), F32),
                pltpu.VMEM((4 * BLK, LANES), F32),
                pltpu.VMEM((4 * BLK, LANES), F32),
                pltpu.VMEM((BOUND, LANES), F32),
                pltpu.VMEM((BOUND, LANES), F32),
                pltpu.SemaphoreType.DMA((4,)),
            ],
            input_output_aliases={5: 0},
            compiler_params=pltpu.CompilerParams(vmem_limit_bytes=40 * 1024 * 1024),
            cost_estimate=pl.CostEstimate(flops=2 * 10**9, bytes_accessed=2 * 10**7, transcendentals=0),
            name=f"edge{stage}",
        )(*args)
        lam, edge = outs[:2]
        arrived = exchange(outs[2:])
        lams.append(lam)

        args = [idx_in, flag_in, block_level, geo, lam]
        specs = [SMEM, SMEM, SMEM, VMEM, VMEM]
        if fwd:
            args += [state, edge]
            specs += [VMEM, VMEM]
        args += [lift_back, own_back, trace_back, trace_fwd, all_fwd]
        specs += [VMEM] * 5
        outs = pl.pallas_call(
            functools.partial(interior_kernel, lowest, fwd, elements),
            out_shape=(row, row) if fwd else (row,),
            in_specs=specs,
            out_specs=(VMEM, VMEM) if fwd else (VMEM,),
            scratch_shapes=[
                pltpu.VMEM((4 * elements + SPREAD, LANES), F32),
                pltpu.VMEM((4 * elements + SPREAD, LANES), F32),
                pltpu.VMEM((4 * BLK, LANES), F32),
                pltpu.VMEM((4 * BLK, LANES), F32),
            ],
            compiler_params=pltpu.CompilerParams(vmem_limit_bytes=48 * 1024 * 1024),
            cost_estimate=pl.CostEstimate(flops=10**10, bytes_accessed=10**8, transcendentals=0),
            name=f"inner{stage}",
        )(*args)
        lam = outs[0]
        if fwd:
            state = outs[1]
            states.append(state)

    part = pl.BlockSpec((1, BLK, LANES), lambda b: (1, jnp.minimum(b, BB - 1), 0))
    adjoint, gradient = pl.pallas_call(
        final_kernel,
        grid=(blocks,),
        out_shape=(
            jax.ShapeDtypeStruct((width, elements), F32),
            jax.ShapeDtypeStruct((1, elements), F32),
        ),
        in_specs=[SMEM] + [part] * 4 + [block] * 9,
        out_specs=(column, pl.BlockSpec((1, BLK), lambda b: (0, b))),
        scratch_shapes=[pltpu.VMEM((BLK, LANES), F32)],
        name="final",
    )(block_level, *arrived, lam, *lams[::-1], *states)
    return adjoint, gradient.reshape(-1)


def solution(mesh):
    in_specs = (
        P(None, ("slab", "dom")),
        P(None, ("slab", "dom")),
        P(("slab", "dom")),
        P(("slab", "dom")),
        P(("slab", "dom")),
        P(None, ("slab", "dom")),
        P(),
        P(),
        P(),
    )
    out_specs = (P(None, ("slab", "dom")), P(("slab", "dom")))
    return jax.shard_map(local, mesh=mesh, in_specs=in_specs, out_specs=out_specs, check_vma=False)
```

```python
import functools

import jax
import jax.numpy as jnp
from jax import lax
from jax.experimental import pallas as pl
from jax.experimental.pallas import tpu as pltpu
from jax.sharding import PartitionSpec as P

BLK = 256
BOUND = 1024
CHUNK = BOUND
PER = CHUNK // BLK
LANES = 128
HALF = 64
UNROLL = BLK
LINE = 128
SPREAD = 64
F32 = jnp.float32
BF16 = jnp.bfloat16

base_step = 0.05
lowest_level = (2, 1, 2, 0)

SMEM = pl.BlockSpec(memory_space=pltpu.SMEM)
VMEM = pl.BlockSpec(memory_space=pltpu.VMEM)
ANY = pl.BlockSpec(memory_space=pl.ANY)


def mm(a, b, dims=((1,), (0,))):
    return lax.dot_general(a, b, (dims, ((), ())), preferred_element_type=F32)


def block_step(level, lowest):
    size = jnp.where(
        level == 2, base_step, jnp.where(level == 1, 2.0 * base_step, 4.0 * base_step)
    )
    return jnp.where(level >= lowest, size, 0.0).astype(F32)


def chunk_step(level_ref, c, lowest):
    parts = [
        jnp.full((BLK, LANES), block_step(level_ref[c * PER + i], lowest), F32) for i in range(PER)
    ]
    return jnp.concatenate(parts, axis=0)


def active_blocks(level_ref, blocks, lowest):
    count = jnp.int32(0)
    for b in range(blocks):
        count = count + jnp.where(level_ref[b] >= lowest, 1, 0)
    return count


def rows_of(c):
    return pl.ds(pl.multiple_of(c * CHUNK, CHUNK), CHUNK)


def move_rows(idx_ref, flag_ref, c, count, source, accs, p_ref, g_ref):
    lines = idx_ref.shape[0] // 4

    def group(q, _):
        face = q & 3
        block = q >> 2
        line = face * lines + c * (CHUNK // LINE) + block * (BLK // LINE)
        pos = pl.multiple_of(face * CHUNK + block * BLK, BLK)

        def fast():
            for t in range(UNROLL // 4):
                acc = accs[t % 2]
                ii = [idx_ref[line + 4 * t // LINE, 4 * t % LINE + r] for r in range(4)]
                vals = [acc[pl.ds(i, 1), :] for i in ii]
                if g_ref is not None:
                    for r in range(4):
                        got = vals[r] if source is None else source[pl.ds(ii[r], 1), :]
                        g_ref[pl.ds(pos + 4 * t + r, 1), :] = got
                for r in range(4):
                    acc[pl.ds(ii[r], 1), :] = vals[r] + p_ref[pl.ds(pos + 4 * t + r, 1), :]

        def slow():
            def some(n, _):
                first = n * 16
                at = line + (n >> 3)
                for r in range(16):
                    acc = accs[r % 2]
                    i = idx_ref[at, (first & (LINE - 1)) + r]
                    val = acc[pl.ds(i, 1), :]
                    if g_ref is not None:
                        got = val if source is None else source[pl.ds(i, 1), :]
                        g_ref[pl.ds(pos + first + r, 1), :] = got
                    acc[pl.ds(i, 1), :] = val + p_ref[pl.ds(pos + first + r, 1), :]
                return 0

            lax.fori_loop(0, UNROLL // 16, some, 0)

        clash = flag_ref[face, c * PER + block]
        pl.when(clash == 0)(fast)
        pl.when(clash != 0)(slow)
        return 0

    lax.fori_loop(0, count * 4, group, 0)


def setup_kernel(
    link_ref, jac_ref, cond_ref, stiff_ref, lift_ref, trace_ref,
    row_out, slot_out, flag_in, flag_edge, small_out,
    trace_fwd, trace_back, lift_back, own_back, all_fwd,
    edge_back, edge_fwd, dup_ref,
):
    width, face_rows = lift_ref.shape
    nodes = face_rows // 4
    elements = link_ref.shape[1]

    code = link_ref[...]
    face = code % 4
    slot = code // 4
    place = lax.broadcasted_iota(jnp.int32, code.shape, 1)
    row = jnp.where(slot < elements, face * elements + slot, 4 * elements + place % SPREAD)
    for table, out in ((row, row_out), (slot, slot_out)):
        lines = out.shape[0] // 4
        for g in range(lines):
            out[pl.ds(g, 4, stride=lines), :] = table[:, g * LINE : (g + 1) * LINE]
    small_out[...] = jnp.zeros_like(small_out)
    small_out[0:1, :] = jac_ref[...]
    small_out[1:2, :] = cond_ref[...]
    small_out[2:6, :] = face.astype(F32)

    def flags(table, out):
        count = table.shape[1]
        at = lax.broadcasted_iota(jnp.int32, table.shape, 1)
        dup = jnp.zeros(table.shape, F32)
        for d in range(1, 4):
            moved = pltpu.roll(table, d, 1)
            dup = jnp.where((table == moved) & (at % 4 >= d), 1.0, dup)
        dup_ref[...] = jnp.zeros_like(dup_ref)
        dup_ref[0:4, 0:count] = dup
        first = lax.broadcasted_iota(jnp.int32, (count, LANES), 0) // UNROLL
        second = lax.broadcasted_iota(jnp.int32, (count, LANES), 1)
        pick = jnp.where(first == second, 1.0, 0.0).astype(BF16)
        total = mm(dup_ref[:, 0:count].astype(BF16), pick)
        out[...] = total.astype(jnp.int32)

    flags(row, flag_in)
    flags(slot[:, :BOUND], flag_edge)

    def pick(rows, columns, lane, group, face_of):
        r = lax.broadcasted_iota(jnp.int32, (rows, columns), 0)
        c = lax.broadcasted_iota(jnp.int32, (rows, columns), 1)
        q = c % group - lane
        hit = (r == 4 * q + face_of(c // group)) & (q >= 0) & (q < nodes)
        return jnp.where(hit, 1.0, 0.0).astype(BF16)

    def put(ref, value, at=None):
        value = value.astype(BF16)
        rows, columns = value.shape
        if at is None:
            ref[...] = jnp.zeros_like(ref)
            at = 0
        ref[at : at + rows, 0:columns] = value

    lift = lift_ref[...]
    trace = trace_ref[...]
    stiff = stiff_ref[...]
    low = pick(face_rows, 4 * LANES, 0, LANES, lambda g: g)
    high = pick(face_rows, 4 * LANES, HALF, LANES, lambda g: g)
    put(trace_fwd, mm(trace, low, ((0,), (0,))))
    put(trace_back, mm(high, trace, ((0,), (0,))))
    put(lift_back, mm(lift, high))
    put(all_fwd, mm(low, lift, ((0,), (1,))))
    edge_back[...] = jnp.zeros_like(edge_back)
    edge_fwd[...] = jnp.zeros_like(edge_fwd)
    one_face = [pick(face_rows, HALF, 0, HALF, lambda g, j=j: j) for j in range(4)]
    lifts = [mm(lift, one_face[j]).astype(BF16) for j in range(4)]
    traces = [mm(one_face[k], trace, ((0,), (0,))).astype(BF16) for k in range(4)]
    for j in range(4):
        for k in range(4):
            at = k * LANES
            edge_back[j, 0:width, at : at + width] = mm(lifts[j], traces[k]).astype(BF16)
            put(edge_fwd, mm(traces[k], lifts[j], ((0,), (1,))), 4 * j * LANES + at)
    own = stiff.astype(F32) - mm(lift, trace)
    r = lax.broadcasted_iota(jnp.int32, (width, width), 0)
    c = lax.broadcasted_iota(jnp.int32, (width, width), 1)
    unit = jnp.where(r == c, 1.0, 0.0).astype(BF16)
    turned = mm(unit, stiff, ((1,), (1,))) - mm(trace, lift, ((0,), (1,)))
    put(own_back, own)
    put(own_back, own - own.astype(BF16).astype(F32), LANES)
    for ref, at in ((all_fwd, 4 * LANES), (edge_fwd, 16 * LANES)):
        put(ref, turned, at)
        put(ref, turned - turned.astype(BF16).astype(F32), at + LANES)


def prep_kernel(x_ref, c_ref, s_ref, u_out, lam_out, geo_out, buf):
    width, elements = x_ref.shape
    buf[...] = jnp.zeros_like(buf)

    def turn(c, _):
        at = pl.ds(pl.multiple_of(c * CHUNK, CHUNK), CHUNK)
        buf[:width, :] = x_ref[:, at]
        u_out[at, :] = buf[...].T
        buf[:width, :] = c_ref[:, at]
        lam_out[at, :] = buf[...].T
        geo_out[at, :] = jnp.concatenate(
            [s_ref[:, at].T, jnp.zeros((CHUNK, LANES - s_ref.shape[0]), F32)], axis=1
        )
        return 0

    lax.fori_loop(0, elements // CHUNK, turn, 0)


def boundary_kernel(stage, elements, *refs):
    fwd = stage > 0
    lowest = lowest_level[3 - stage]
    refs = list(refs)
    idx_ref, flag_ref, level_ref, side_ref, geo_ref, u_ref, lam_ref = refs[:7]
    del refs[:7]
    arrived = []
    if fwd:
        arrived = refs[:4]
        del refs[:4]
    back_ops, fwd_ops = refs[:2]
    lam_out, u_out, own_out = refs[2:5]
    sends = refs[5:9]
    ubuf, acc0, acc1, p_ref, g_ref, sem = refs[9:]
    active = jnp.minimum(active_blocks(level_ref, PER, lowest), PER)
    up_slab, up_dom = side_ref[0], side_ref[1]
    regions = (up_slab, 1 - up_slab, 2 + up_dom, 3 - up_dom)

    def region(r):
        return pl.ds(pl.multiple_of(elements + regions[r] * BOUND, BOUND), BOUND)

    if fwd:
        copy = pltpu.make_async_copy(u_ref, ubuf.at[pl.ds(0, elements)], sem)
        copy.start()
        for r in range(4):
            ubuf[region(r), :] = arrived[r][1].astype(F32)
        g_ref[...] = jnp.zeros_like(g_ref)
    acc0[...] = jnp.zeros_like(acc0)
    acc1[...] = jnp.zeros_like(acc1)

    lam = lam_ref[0:BOUND, :]
    for a in arrived:
        lam = lam + a[0].astype(F32)
    lam_out[...] = lam
    geo = geo_ref[0:BOUND, :]
    weighted = (geo[:, 0:1] * (chunk_step(level_ref, 0, lowest) * lam)).astype(BF16)
    for j in range(4):
        face = jnp.broadcast_to(geo_ref[0:BOUND, 2 + j : 3 + j], (BOUND, LANES))
        every = mm(weighted, back_ops[j])
        part = every[:, 0:LANES]
        for k in range(1, 4):
            part = jnp.where(face == k, every[:, k * LANES : (k + 1) * LANES], part)
        p_ref[j * BOUND : (j + 1) * BOUND, :] = part
    if fwd:
        copy.wait()
    move_rows(idx_ref, flag_ref, 0, active, ubuf, (acc0, acc1), p_ref, g_ref if fwd else None)
    u = u_ref[0:BOUND, :]
    if fwd:
        low = u.astype(BF16)
        change = mm(jnp.concatenate([low, low], axis=1), fwd_ops[16 * LANES :, :])
        for j in range(4):
            face = jnp.broadcast_to(geo_ref[0:BOUND, 2 + j : 3 + j], (BOUND, LANES))
            got = g_ref[j * BOUND : (j + 1) * BOUND, :]
            parts = [jnp.where(face == k, got, 0.0).astype(BF16) for k in range(4)]
            change = change + mm(
                jnp.concatenate(parts, axis=1), fwd_ops[4 * j * LANES : 4 * (j + 1) * LANES, :]
            )
        geo = geo_ref[0:BOUND, :]
        u = u + chunk_step(level_ref, 0, lowest) * (geo[:, 0:1] * change - geo[:, 1:2] * u)
    u_out[...] = u
    for r in range(4):
        sends[r][0] = (acc0[region(r), :] + acc1[region(r), :]).astype(BF16)
        if stage < 3:
            sends[r][1] = u_out[...].astype(BF16)

    def total(c, _):
        own_out[rows_of(c), :] = acc0[rows_of(c), :] + acc1[rows_of(c), :]
        return 0

    lax.fori_loop(0, elements // CHUNK, total, 0)


def interior_kernel(stage, elements, *refs):
    fwd = stage > 0
    lowest = lowest_level[3 - stage]
    refs = list(refs)
    idx_ref, flag_ref, level_ref, geo_ref, lam_ref, edge_lam, edge_own = refs[:7]
    del refs[:7]
    if fwd:
        u_ref, edge_u = refs[:2]
        del refs[:2]
    extra = []
    if stage == 2:
        edge_lam3 = refs.pop(0)
        extra = [refs.pop(0)]
    if stage == 3:
        extra = refs[:3]
        del refs[:3]
    lift_back, own_back, trace_back, trace_fwd, all_fwd = refs[:5]
    del refs[:5]
    lam_out = refs.pop(0)
    if stage >= 2:
        q_out = refs.pop(0)
    if fwd:
        u_out = refs.pop(0)
    tab0, tab1, p_ref, g_ref = refs[:4]
    if extra:
        held, sems = refs[4:]
    chunks = elements // CHUNK
    active = active_blocks(level_ref, level_ref.shape[0], lowest)
    busy_chunks = (active + (PER - 1)) // PER

    def plane(c, k):
        return pl.ds(pl.multiple_of(k * elements + c * CHUNK, CHUNK), CHUNK)

    def fetch(c):
        return [
            pltpu.make_async_copy(ref.at[pl.ds(c * CHUNK, CHUNK)], held.at[c % 2, i], sems.at[c % 2, i])
            for i, ref in enumerate(extra)
        ]

    for copy in fetch(0):
        copy.start()

    def start(c, _):
        if fwd:
            traces = mm(u_ref[rows_of(c), :].astype(BF16), trace_fwd[...])
            traces = traces.astype(BF16).astype(F32)
        for k in range(4):
            part = traces[:, k * LANES : (k + 1) * LANES] if fwd else jnp.zeros((CHUNK, LANES), F32)
            tab0[plane(c, k), :] = part
            tab1[plane(c, k), :] = part
        return 0

    lax.fori_loop(0, chunks, start, 0)
    if fwd:
        g_ref[...] = jnp.zeros_like(g_ref)

    def adjoint(c, lam, links):
        geo = geo_ref[rows_of(c), :]
        scaled = chunk_step(level_ref, c, lowest) * lam
        weighted = (geo[:, 0:1] * scaled).astype(BF16)
        if links:
            lifted = mm(weighted, lift_back[...])
            for j in range(4):
                p_ref[j * CHUNK : (j + 1) * CHUNK, :] = lifted[:, j * LANES : (j + 1) * LANES]
        own = mm(jnp.concatenate([weighted, weighted], axis=1), own_back[...])
        lam_out[rows_of(c), :] = lam - geo[:, 1:2] * scaled + own

    tabs = (tab0, tab1)
    adjoint(0, edge_lam[...], False)
    if fwd:
        u_out[0:CHUNK, :] = edge_u[...]

    def busy(c, _):
        adjoint(c, lam_ref[rows_of(c), :], True)
        count = jnp.minimum(active - c * PER, PER)
        move_rows(idx_ref, flag_ref, c, count, None, tabs, p_ref, g_ref if fwd else None)
        if fwd:
            geo = geo_ref[rows_of(c), :]
            u = u_ref[rows_of(c), :]
            low = u.astype(BF16)
            parts = [g_ref[j * CHUNK : (j + 1) * CHUNK, :].astype(BF16) for j in range(4)]
            change = mm(jnp.concatenate(parts + [low, low], axis=1), all_fwd[...])
            step = chunk_step(level_ref, c, lowest)
            u_out[rows_of(c), :] = u + step * (geo[:, 0:1] * change - geo[:, 1:2] * u)
        return 0

    def idle(c, _):
        lam_out[rows_of(c), :] = lam_ref[rows_of(c), :]
        if fwd:
            u_out[rows_of(c), :] = u_ref[rows_of(c), :]
        return 0

    lax.fori_loop(1, busy_chunks, busy, 0)
    lax.fori_loop(busy_chunks, chunks, idle, 0)

    def collect(c):
        parts = [
            (tab0[plane(c, k), :] + tab1[plane(c, k), :]).astype(BF16) for k in range(4)
        ]
        back = mm(jnp.concatenate(parts, axis=1), trace_back[...])
        at = rows_of(c)
        lam_out[at, :] = lam_out[at, :] + edge_own[at, :] + back

    def multiply(c):
        at = rows_of(c)
        lam = edge_lam[...] if c == 0 else lam_ref[at, :]

        def step(s):
            return chunk_step(level_ref, c, lowest_level[s])

        if stage == 2:
            lam3 = edge_lam3[...] if c == 0 else held[c % 2, 0]
            q_out[at, :] = (step(1) * lam) * u_ref[at, :] + (step(2) * lam3) * u_out[at, :]
        else:
            u0, lam4, before = (held[c % 2, i] for i in range(3))
            q_out[at, :] = before + (step(0) * lam) * u0 + (step(3) * lam4) * u_out[at, :]

    if not extra:
        lax.fori_loop(0, chunks, lambda c, _: (collect(c), 0)[1], 0)
        return
    for c in range(chunks):
        if c + 1 < chunks:
            for copy in fetch(c + 1):
                copy.start()
        collect(c)
        for copy in fetch(c):
            copy.wait()
        multiply(c)


def final_kernel(*refs):
    arrived = refs[:4]
    lam_ref, q_ref, adj_out, grad_out, buf = refs[4:]
    buf[...] = lam_ref[...]

    @pl.when(pl.program_id(0) == 0)
    def _():
        total = lam_ref[...]
        for a in arrived:
            total = total + a[0].astype(F32)
        buf[...] = total

    adj_out[...] = buf[...].T[: adj_out.shape[0], :]
    grad_out[...] = -jnp.sum(q_ref[...].T, axis=0, keepdims=True)


def exchange(parts):
    out = []
    for part, axis, odd in zip(parts, ("slab", "slab", "dom", "dom"), (0, 1, 0, 1), strict=True):
        pairs = []
        for i in range(odd, lax.axis_size(axis) - 1, 2):
            pairs += [(i, i + 1), (i + 1, i)]
        out.append(lax.ppermute(part, axis, pairs))
    return out


def local(
    initial_field, cotangent, jacobian, conductivity, block_level, face_link, stiff, lift, trace_op
):
    width, elements = initial_field.shape
    chunks = elements // CHUNK
    shape = jax.ShapeDtypeStruct
    square = shape((LANES, 4 * LANES), BF16)

    (
        idx_in, slots, flag_in, flag_edge, small,
        trace_fwd, trace_back, lift_back, own_back, all_fwd, edge_back, edge_fwd,
    ) = pl.pallas_call(
        setup_kernel,
        out_shape=(
            shape((4 * elements // LINE, LINE), jnp.int32),
            shape((4 * BOUND // LINE, LINE), jnp.int32),
            shape((8, LANES), jnp.int32),
            shape((8, LANES), jnp.int32),
            shape((8, elements), F32),
            square,
            shape((4 * LANES, LANES), BF16),
            square,
            shape((2 * LANES, LANES), BF16),
            shape((6 * LANES, LANES), BF16),
            shape((4, LANES, 4 * LANES), BF16),
            shape((18 * LANES, LANES), BF16),
        ),
        in_specs=[VMEM] * 6,
        out_specs=(VMEM,) * 12,
        scratch_shapes=[pltpu.VMEM((8, elements), F32)],
        name="setup",
    )(face_link, jacobian.reshape(1, -1), conductivity.reshape(1, -1), stiff, lift, trace_op)
    side = jnp.stack([1 - lax.axis_index("slab") % 2, 1 - lax.axis_index("dom") % 2]).astype(jnp.int32)

    row = shape((elements, LANES), F32)
    edge_row = shape((BOUND, LANES), F32)
    column = pl.BlockSpec((width, CHUNK), lambda c: (0, c))
    block = pl.BlockSpec((CHUNK, LANES), lambda c: (c, 0))

    state, lam, geo = pl.pallas_call(
        prep_kernel,
        out_shape=(row, row, row),
        in_specs=[VMEM] * 3,
        out_specs=(VMEM,) * 3,
        scratch_shapes=[pltpu.VMEM((LANES, CHUNK), F32)],
        compiler_params=pltpu.CompilerParams(vmem_limit_bytes=16 * 1024 * 1024),
        name="prep",
    )(initial_field, cotangent, small)

    buffer_len = elements + 4 * BOUND
    arrived = []
    state0, lam4 = state, lam
    for stage in range(4):
        fwd = stage > 0
        args = [slots, flag_edge, block_level, side, geo, state, lam, *arrived, edge_back, edge_fwd]
        payload = shape((2 if stage < 3 else 1, BOUND, LANES), BF16)
        outs = pl.pallas_call(
            functools.partial(boundary_kernel, stage, elements),
            out_shape=(edge_row, edge_row, row) + (payload,) * 4,
            in_specs=[SMEM] * 4 + [VMEM] * (len(args) - 4),
            out_specs=(VMEM,) * 7,
            scratch_shapes=[
                pltpu.VMEM((buffer_len, LANES), F32),
                pltpu.VMEM((buffer_len, LANES), F32),
                pltpu.VMEM((buffer_len, LANES), F32),
                pltpu.VMEM((4 * CHUNK, LANES), F32),
                pltpu.VMEM((4 * CHUNK, LANES), F32),
                pltpu.SemaphoreType.DMA,
            ],
            compiler_params=pltpu.CompilerParams(vmem_limit_bytes=26 * 1024 * 1024),
            cost_estimate=pl.CostEstimate(flops=2 * 10**9, bytes_accessed=2 * 10**7, transcendentals=0),
            name=f"edge{stage}",
        )(*args)
        edge_lam, edge_u, edge_own = outs[:3]
        arrived = exchange(outs[3:])

        args = [idx_in, flag_in, block_level, geo, lam, edge_lam, edge_own]
        if fwd:
            args += [state, edge_u]
        extra = []
        if stage == 2:
            args += [edge_lam3]
            extra = [lam3]
        if stage == 3:
            extra = [state0, lam4, products]
        plain = len(args) - 3
        args += extra + [lift_back, own_back, trace_back, trace_fwd, all_fwd]
        count = (1, 2, 3, 2)[stage]
        scratch = [
            pltpu.VMEM((4 * elements + SPREAD, LANES), F32),
            pltpu.VMEM((4 * elements + SPREAD, LANES), F32),
            pltpu.VMEM((4 * CHUNK, LANES), F32),
            pltpu.VMEM((4 * CHUNK, LANES), F32),
        ]
        if stage == 3:
            scratch.insert(0, pltpu.VMEM((elements, LANES), F32))
        if extra:
            scratch += [
                pltpu.VMEM((2, len(extra), CHUNK, LANES), F32),
                pltpu.SemaphoreType.DMA((2, len(extra))),
            ]
        if stage == 1:
            lam3, edge_lam3 = lam, edge_lam
        outs = pl.pallas_call(
            functools.partial(interior_kernel, stage, elements),
            out_shape=(row,) * count,
            in_specs=[SMEM] * 3 + [VMEM] * plain + [ANY] * len(extra) + [VMEM] * 5,
            out_specs=(VMEM,) * count,
            scratch_shapes=scratch,
            compiler_params=pltpu.CompilerParams(vmem_limit_bytes=(30, 30, 34, 38)[stage] * 1024 * 1024),
            cost_estimate=pl.CostEstimate(flops=10**10, bytes_accessed=10**8, transcendentals=0),
            name=f"inner{stage}",
        )(*args)
        lam = outs[0]
        if stage > 1:
            products = outs[1]
        if fwd and stage < 3:
            state = outs[-1]

    part = pl.BlockSpec((1, BOUND, LANES), lambda c: (0, 0, 0))
    adjoint, gradient = pl.pallas_call(
        final_kernel,
        grid=(chunks,),
        out_shape=(shape((width, elements), F32), shape((1, elements), F32)),
        in_specs=[part] * 4 + [block] * 2,
        out_specs=(column, pl.BlockSpec((1, CHUNK), lambda c: (0, c))),
        scratch_shapes=[pltpu.VMEM((CHUNK, LANES), F32)],
        name="final",
    )(*arrived, lam, products)
    return adjoint, gradient.reshape(-1)


def solution(mesh):
    in_specs = (
        P(None, ("slab", "dom")),
        P(None, ("slab", "dom")),
        P(("slab", "dom")),
        P(("slab", "dom")),
        P(("slab", "dom")),
        P(None, ("slab", "dom")),
        P(),
        P(),
        P(),
    )
    out_specs = (P(None, ("slab", "dom")), P(("slab", "dom")))
    return jax.shard_map(local, mesh=mesh, in_specs=in_specs, out_specs=out_specs, check_vma=False)
```

```python
import functools

import jax
import jax.numpy as jnp
from jax import lax
from jax.experimental import pallas as pl
from jax.experimental.pallas import tpu as pltpu
from jax.sharding import PartitionSpec as P

BLK = 256
BOUND = 1024
CHUNK = BOUND
PER = CHUNK // BLK
LANES = 128
HALF = 64
UNROLL = BLK
LINE = 128
SPREAD = 64
F32 = jnp.float32
BF16 = jnp.bfloat16

base_step = 0.05
lowest_level = (2, 1, 2, 0)

SMEM = pl.BlockSpec(memory_space=pltpu.SMEM)
VMEM = pl.BlockSpec(memory_space=pltpu.VMEM)
ANY = pl.BlockSpec(memory_space=pl.ANY)
HBM = pl.BlockSpec(memory_space=pltpu.HBM)


def mm(a, b, dims=((1,), (0,))):
    return lax.dot_general(a, b, (dims, ((), ())), preferred_element_type=F32)


def block_step(level, lowest):
    size = jnp.where(
        level == 2, base_step, jnp.where(level == 1, 2.0 * base_step, 4.0 * base_step)
    )
    return jnp.where(level >= lowest, size, 0.0).astype(F32)


def chunk_step(level_ref, c, lowest):
    parts = [
        jnp.full((BLK, LANES), block_step(level_ref[c * PER + i], lowest), F32) for i in range(PER)
    ]
    return jnp.concatenate(parts, axis=0)


def active_blocks(level_ref, blocks, lowest):
    count = jnp.int32(0)
    for b in range(blocks):
        count = count + jnp.where(level_ref[b] >= lowest, 1, 0)
    return count


def rows_of(c):
    return pl.ds(pl.multiple_of(c * CHUNK, CHUNK), CHUNK)


def move_rows(idx_ref, flag_ref, c, count, source, accs, p_ref, g_ref):
    lines = idx_ref.shape[0] // 4

    def group(q, _):
        face = q & 3
        block = q >> 2
        line = face * lines + c * (CHUNK // LINE) + block * (BLK // LINE)
        pos = pl.multiple_of(face * CHUNK + block * BLK, BLK)

        def fast():
            for t in range(UNROLL // 4):
                acc = accs[t % 2]
                ii = [idx_ref[line + 4 * t // LINE, 4 * t % LINE + r] for r in range(4)]
                vals = [acc[pl.ds(i, 1), :] for i in ii]
                if g_ref is not None:
                    for r in range(4):
                        got = vals[r] if source is None else source[pl.ds(ii[r], 1), :]
                        g_ref[pl.ds(pos + 4 * t + r, 1), :] = got
                for r in range(4):
                    acc[pl.ds(ii[r], 1), :] = vals[r] + p_ref[pl.ds(pos + 4 * t + r, 1), :]

        def slow():
            def some(n, _):
                first = n * 16
                at = line + (n >> 3)
                for r in range(16):
                    acc = accs[r % 2]
                    i = idx_ref[at, (first & (LINE - 1)) + r]
                    val = acc[pl.ds(i, 1), :]
                    if g_ref is not None:
                        got = val if source is None else source[pl.ds(i, 1), :]
                        g_ref[pl.ds(pos + first + r, 1), :] = got
                    acc[pl.ds(i, 1), :] = val + p_ref[pl.ds(pos + first + r, 1), :]
                return 0

            lax.fori_loop(0, UNROLL // 16, some, 0)

        clash = flag_ref[face, c * PER + block]
        pl.when(clash == 0)(fast)
        pl.when(clash != 0)(slow)
        return 0

    lax.fori_loop(0, count * 4, group, 0)


def setup_kernel(
    link_ref, jac_ref, cond_ref, stiff_ref, lift_ref, trace_ref,
    row_out, slot_out, flag_in, flag_edge, small_out,
    trace_fwd, trace_back, lift_back, own_back, all_fwd,
    edge_back, edge_fwd, dup_ref,
):
    face_rows, width = lift_ref.shape
    nodes = face_rows // 4
    elements = link_ref.shape[1]

    code = link_ref[...]
    face = code % 4
    slot = code // 4
    place = lax.broadcasted_iota(jnp.int32, code.shape, 1)
    row = jnp.where(slot < elements, face * elements + slot, 4 * elements + place % SPREAD)
    for table, out in ((row, row_out), (slot, slot_out)):
        lines = out.shape[0] // 4
        for g in range(lines):
            out[pl.ds(g, 4, stride=lines), :] = table[:, g * LINE : (g + 1) * LINE]
    small_out[...] = jnp.zeros_like(small_out)
    small_out[0:1, :] = jac_ref[...]
    small_out[1:2, :] = cond_ref[...]
    small_out[2:6, :] = face.astype(F32)

    def flags(table, out):
        count = table.shape[1]
        at = lax.broadcasted_iota(jnp.int32, table.shape, 1)
        dup = jnp.zeros(table.shape, F32)
        for d in range(1, 4):
            moved = pltpu.roll(table, d, 1)
            dup = jnp.where((table == moved) & (at % 4 >= d), 1.0, dup)
        dup_ref[...] = jnp.zeros_like(dup_ref)
        dup_ref[0:4, 0:count] = dup
        first = lax.broadcasted_iota(jnp.int32, (count, LANES), 0) // UNROLL
        second = lax.broadcasted_iota(jnp.int32, (count, LANES), 1)
        pick = jnp.where(first == second, 1.0, 0.0).astype(BF16)
        total = mm(dup_ref[:, 0:count].astype(BF16), pick)
        out[...] = total.astype(jnp.int32)

    flags(row, flag_in)
    flags(slot[:, :BOUND], flag_edge)

    def pick(rows, columns, lane, group, face_of):
        r = lax.broadcasted_iota(jnp.int32, (rows, columns), 0)
        c = lax.broadcasted_iota(jnp.int32, (rows, columns), 1)
        q = c % group - lane
        hit = (r == 4 * q + face_of(c // group)) & (q >= 0) & (q < nodes)
        return jnp.where(hit, 1.0, 0.0).astype(BF16)

    def put(ref, value, at=None):
        value = value.astype(BF16)
        rows, columns = value.shape
        if at is None:
            ref[...] = jnp.zeros_like(ref)
            at = 0
        ref[at : at + rows, 0:columns] = value

    lift = lift_ref[...]
    trace = trace_ref[...]
    stiff = stiff_ref[...]
    low = pick(face_rows, 4 * LANES, 0, LANES, lambda g: g)
    high = pick(face_rows, 4 * LANES, HALF, LANES, lambda g: g)
    put(trace_fwd, mm(trace, low, ((0,), (0,))))
    put(trace_back, mm(high, trace, ((0,), (0,))))
    put(lift_back, mm(lift, high, ((0,), (0,))))
    put(all_fwd, mm(low, lift, ((0,), (0,))))
    edge_back[...] = jnp.zeros_like(edge_back)
    edge_fwd[...] = jnp.zeros_like(edge_fwd)
    one_face = [pick(face_rows, HALF, 0, HALF, lambda g, j=j: j) for j in range(4)]
    lifts = [mm(lift, one_face[j], ((0,), (0,))).astype(BF16) for j in range(4)]
    traces = [mm(one_face[k], trace, ((0,), (0,))).astype(BF16) for k in range(4)]
    for j in range(4):
        for k in range(4):
            at = k * LANES
            edge_back[j, 0:width, at : at + width] = mm(lifts[j], traces[k]).astype(BF16)
            put(edge_fwd, mm(traces[k], lifts[j], ((0,), (1,))), 4 * j * LANES + at)
    own = stiff.astype(F32) - mm(lift, trace, ((0,), (0,)))
    r = lax.broadcasted_iota(jnp.int32, (width, width), 0)
    c = lax.broadcasted_iota(jnp.int32, (width, width), 1)
    unit = jnp.where(r == c, 1.0, 0.0).astype(BF16)
    turned = mm(unit, stiff, ((1,), (1,))) - mm(trace, lift, ((0,), (0,)))
    put(own_back, own)
    put(own_back, own - own.astype(BF16).astype(F32), LANES)
    for ref, at in ((all_fwd, 4 * LANES), (edge_fwd, 16 * LANES)):
        put(ref, turned, at)
        put(ref, turned - turned.astype(BF16).astype(F32), at + LANES)


def prep_kernel(x_ref, c_ref, s_ref, u_out, lam_out, geo_out, buf):
    width, elements = x_ref.shape
    buf[...] = jnp.zeros_like(buf)

    def turn(c, _):
        at = pl.ds(pl.multiple_of(c * CHUNK, CHUNK), CHUNK)
        buf[:width, :] = x_ref[:, at]
        u_out[at, :] = buf[...].T
        buf[:width, :] = c_ref[:, at]
        lam_out[at, :] = buf[...].T
        geo_out[at, :] = jnp.concatenate(
            [s_ref[:, at].T, jnp.zeros((CHUNK, LANES - s_ref.shape[0]), F32)], axis=1
        )
        return 0

    lax.fori_loop(0, elements // CHUNK, turn, 0)


def boundary_kernel(stage, elements, *refs):
    fwd = stage > 0
    lowest = lowest_level[3 - stage]
    refs = list(refs)
    idx_ref, flag_ref, level_ref, side_ref, geo_ref, u_ref, lam_ref = refs[:7]
    del refs[:7]
    arrived = []
    if fwd:
        arrived = refs[:4]
        del refs[:4]
    back_ops, fwd_ops = refs[:2]
    lam_out, u_out, own_out = refs[2:5]
    sends = refs[5:9]
    ubuf, acc0, acc1, p_ref, g_ref, sem = refs[9:]
    active = jnp.minimum(active_blocks(level_ref, PER, lowest), PER)
    up_slab, up_dom = side_ref[0], side_ref[1]
    regions = (up_slab, 1 - up_slab, 2 + up_dom, 3 - up_dom)

    def region(r):
        return pl.ds(pl.multiple_of(elements + regions[r] * BOUND, BOUND), BOUND)

    if fwd:
        copy = pltpu.make_async_copy(u_ref, ubuf.at[pl.ds(0, elements)], sem)
        copy.start()
        for r in range(4):
            ubuf[region(r), :] = arrived[r][1].astype(F32)
        g_ref[...] = jnp.zeros_like(g_ref)
    acc0[...] = jnp.zeros_like(acc0)
    acc1[...] = jnp.zeros_like(acc1)

    lam = lam_ref[0:BOUND, :]
    for a in arrived:
        lam = lam + a[0].astype(F32)
    lam_out[...] = lam
    geo = geo_ref[0:BOUND, :]
    weighted = (geo[:, 0:1] * (chunk_step(level_ref, 0, lowest) * lam)).astype(BF16)
    for j in range(4):
        face = jnp.broadcast_to(geo_ref[0:BOUND, 2 + j : 3 + j], (BOUND, LANES))
        every = mm(weighted, back_ops[j])
        part = every[:, 0:LANES]
        for k in range(1, 4):
            part = jnp.where(face == k, every[:, k * LANES : (k + 1) * LANES], part)
        p_ref[j * BOUND : (j + 1) * BOUND, :] = part
    if fwd:
        copy.wait()
    move_rows(idx_ref, flag_ref, 0, active, ubuf, (acc0, acc1), p_ref, g_ref if fwd else None)
    u = u_ref[0:BOUND, :]
    if fwd:
        low = u.astype(BF16)
        change = mm(jnp.concatenate([low, low], axis=1), fwd_ops[16 * LANES :, :])
        for j in range(4):
            face = jnp.broadcast_to(geo_ref[0:BOUND, 2 + j : 3 + j], (BOUND, LANES))
            got = g_ref[j * BOUND : (j + 1) * BOUND, :]
            parts = [jnp.where(face == k, got, 0.0).astype(BF16) for k in range(4)]
            change = change + mm(
                jnp.concatenate(parts, axis=1), fwd_ops[4 * j * LANES : 4 * (j + 1) * LANES, :]
            )
        geo = geo_ref[0:BOUND, :]
        u = u + chunk_step(level_ref, 0, lowest) * (geo[:, 0:1] * change - geo[:, 1:2] * u)
    u_out[...] = u
    for r in range(4):
        sends[r][0] = (acc0[region(r), :] + acc1[region(r), :]).astype(BF16)
        if stage < 3:
            sends[r][1] = u_out[...].astype(BF16)

    def total(c, _):
        own_out[rows_of(c), :] = acc0[rows_of(c), :] + acc1[rows_of(c), :]
        return 0

    lax.fori_loop(0, elements // CHUNK, total, 0)


def interior_kernel(stage, elements, *refs):
    fwd = stage > 0
    lowest = lowest_level[3 - stage]
    refs = list(refs)
    idx_ref, flag_ref, level_ref, geo_ref, lam_ref, edge_lam, edge_own = refs[:7]
    del refs[:7]
    if fwd:
        u_ref, edge_u = refs[:2]
        del refs[:2]
    extra = []
    if stage == 2:
        edge_lam3 = refs.pop(0)
        extra = [refs.pop(0)]
    if stage == 3:
        extra = refs[:3]
        del refs[:3]
    lift_back, own_back, trace_back, trace_fwd, all_fwd = refs[:5]
    del refs[:5]
    if stage == 3:
        adj_out, grad_out, first_out = refs[:3]
        del refs[:3]
        turned, turn_sems = refs[-2:]
        del refs[-2:]
    lam_out = refs.pop(0)
    if stage == 2:
        q_out = refs.pop(0)
    if fwd:
        u_out = refs.pop(0)
    tab0, tab1, p_ref, g_ref = refs[:4]
    if extra:
        held, sems = refs[4:]
    chunks = elements // CHUNK
    active = active_blocks(level_ref, level_ref.shape[0], lowest)
    busy_chunks = (active + (PER - 1)) // PER

    def plane(c, k):
        return pl.ds(pl.multiple_of(k * elements + c * CHUNK, CHUNK), CHUNK)

    def fetch(c):
        return [
            pltpu.make_async_copy(ref.at[pl.ds(c * CHUNK, CHUNK)], held.at[c % 2, i], sems.at[c % 2, i])
            for i, ref in enumerate(extra)
        ]

    for copy in fetch(0):
        copy.start()

    def start(c, _):
        if fwd:
            traces = mm(u_ref[rows_of(c), :].astype(BF16), trace_fwd[...])
            traces = traces.astype(BF16).astype(F32)
        for k in range(4):
            part = traces[:, k * LANES : (k + 1) * LANES] if fwd else jnp.zeros((CHUNK, LANES), F32)
            tab0[plane(c, k), :] = part
            tab1[plane(c, k), :] = part
        return 0

    lax.fori_loop(0, chunks, start, 0)
    if fwd:
        g_ref[...] = jnp.zeros_like(g_ref)

    def adjoint(c, lam, links):
        geo = geo_ref[rows_of(c), :]
        scaled = chunk_step(level_ref, c, lowest) * lam
        weighted = (geo[:, 0:1] * scaled).astype(BF16)
        if links:
            lifted = mm(weighted, lift_back[...])
            for j in range(4):
                p_ref[j * CHUNK : (j + 1) * CHUNK, :] = lifted[:, j * LANES : (j + 1) * LANES]
        own = mm(jnp.concatenate([weighted, weighted], axis=1), own_back[...])
        lam_out[rows_of(c), :] = lam - geo[:, 1:2] * scaled + own

    tabs = (tab0, tab1)
    adjoint(0, edge_lam[...], False)
    if fwd:
        u_out[0:CHUNK, :] = edge_u[...]

    def busy(c, _):
        adjoint(c, lam_ref[rows_of(c), :], True)
        count = jnp.minimum(active - c * PER, PER)
        move_rows(idx_ref, flag_ref, c, count, None, tabs, p_ref, g_ref if fwd else None)
        if fwd:
            geo = geo_ref[rows_of(c), :]
            u = u_ref[rows_of(c), :]
            low = u.astype(BF16)
            parts = [g_ref[j * CHUNK : (j + 1) * CHUNK, :].astype(BF16) for j in range(4)]
            change = mm(jnp.concatenate(parts + [low, low], axis=1), all_fwd[...])
            step = chunk_step(level_ref, c, lowest)
            u_out[rows_of(c), :] = u + step * (geo[:, 0:1] * change - geo[:, 1:2] * u)
        return 0

    def idle(c, _):
        lam_out[rows_of(c), :] = lam_ref[rows_of(c), :]
        if fwd:
            u_out[rows_of(c), :] = u_ref[rows_of(c), :]
        return 0

    lax.fori_loop(1, busy_chunks, busy, 0)
    lax.fori_loop(busy_chunks, chunks, idle, 0)

    def collect(c):
        parts = [
            (tab0[plane(c, k), :] + tab1[plane(c, k), :]).astype(BF16) for k in range(4)
        ]
        back = mm(jnp.concatenate(parts, axis=1), trace_back[...])
        at = rows_of(c)
        lam_out[at, :] = lam_out[at, :] + edge_own[at, :] + back

    def multiply(c):
        at = rows_of(c)
        lam = edge_lam[...] if c == 0 else lam_ref[at, :]

        def step(s):
            return chunk_step(level_ref, c, lowest_level[s])

        if stage == 2:
            lam3 = edge_lam3[...] if c == 0 else held[c % 2, 0]
            q_out[at, :] = (step(1) * lam) * u_ref[at, :] + (step(2) * lam3) * u_out[at, :]
        else:
            u0, lam4, before = (held[c % 2, i] for i in range(3))
            total = before + (step(0) * lam) * u0 + (step(3) * lam4) * u_out[at, :]
            where = slice(c * CHUNK, (c + 1) * CHUNK)
            grad_out[0:1, where] = -jnp.sum(total.T, axis=0, keepdims=True)
            if c > 0:
                turned[c - 1] = lam_out[at, :].T[: adj_out.shape[0], :]
                store(c).start()
            else:
                first_out[...] = lam_out[at, :]

    def store(c):
        return pltpu.make_async_copy(
            turned.at[c - 1], adj_out.at[:, pl.ds(c * CHUNK, CHUNK)], turn_sems.at[c - 1]
        )

    if not extra:
        lax.fori_loop(0, chunks, lambda c, _: (collect(c), 0)[1], 0)
        return
    for c in range(chunks):
        if c + 1 < chunks:
            for copy in fetch(c + 1):
                copy.start()
        collect(c)
        for copy in fetch(c):
            copy.wait()
        multiply(c)
    if stage == 3:
        for c in range(1, chunks):
            store(c).wait()


def final_kernel(adj_in, first_ref, *refs):
    arrived = refs[:4]
    adj_out, turned, sem = refs[4:]
    del adj_in
    total = first_ref[...]
    for a in arrived:
        total = total + a[0].astype(F32)
    turned[...] = total.T[: turned.shape[0], :]
    store = pltpu.make_async_copy(turned, adj_out.at[:, pl.ds(0, BOUND)], sem)
    store.start()
    store.wait()


def exchange(parts):
    out = []
    for part, axis, odd in zip(parts, ("slab", "slab", "dom", "dom"), (0, 1, 0, 1), strict=True):
        pairs = []
        for i in range(odd, lax.axis_size(axis) - 1, 2):
            pairs += [(i, i + 1), (i + 1, i)]
        out.append(lax.ppermute(part, axis, pairs))
    return out


def local(
    initial_field, cotangent, jacobian, conductivity, block_level, face_link, stiff, lift, trace_op
):
    width, elements = initial_field.shape
    shape = jax.ShapeDtypeStruct
    square = shape((LANES, 4 * LANES), BF16)
    row = shape((elements, LANES), F32)
    edge_row = shape((BOUND, LANES), F32)

    (
        idx_in, slots, flag_in, flag_edge, small,
        trace_fwd, trace_back, lift_back, own_back, all_fwd, edge_back, edge_fwd,
    ) = pl.pallas_call(
        setup_kernel,
        out_shape=(
            shape((4 * elements // LINE, LINE), jnp.int32),
            shape((4 * BOUND // LINE, LINE), jnp.int32),
            shape((8, LANES), jnp.int32),
            shape((8, LANES), jnp.int32),
            shape((8, elements), F32),
            square,
            shape((4 * LANES, LANES), BF16),
            square,
            shape((2 * LANES, LANES), BF16),
            shape((6 * LANES, LANES), BF16),
            shape((4, LANES, 4 * LANES), BF16),
            shape((18 * LANES, LANES), BF16),
        ),
        in_specs=[VMEM] * 6,
        out_specs=(VMEM,) * 12,
        scratch_shapes=[pltpu.VMEM((8, elements), F32)],
        name="setup",
    )(face_link, jacobian.reshape(1, -1), conductivity.reshape(1, -1), stiff, lift.T, trace_op)
    state, lam, geo = pl.pallas_call(
        prep_kernel,
        out_shape=(row, row, row),
        in_specs=[VMEM] * 3,
        out_specs=(VMEM,) * 3,
        scratch_shapes=[pltpu.VMEM((LANES, CHUNK), F32)],
        compiler_params=pltpu.CompilerParams(vmem_limit_bytes=16 * 1024 * 1024),
        name="prep",
    )(initial_field, cotangent, small)
    side = jnp.stack([1 - lax.axis_index("slab") % 2, 1 - lax.axis_index("dom") % 2]).astype(jnp.int32)

    buffer_len = elements + 4 * BOUND
    arrived = []
    state0, lam4 = state, lam
    for stage in range(4):
        fwd = stage > 0
        args = [slots, flag_edge, block_level, side, geo, state, lam, *arrived, edge_back, edge_fwd]
        payload = shape((2 if stage < 3 else 1, BOUND, LANES), BF16)
        outs = pl.pallas_call(
            functools.partial(boundary_kernel, stage, elements),
            out_shape=(edge_row, edge_row, row) + (payload,) * 4,
            in_specs=[SMEM] * 4 + [VMEM] * (len(args) - 4),
            out_specs=(VMEM,) * 7,
            scratch_shapes=[
                pltpu.VMEM((buffer_len, LANES), F32),
                pltpu.VMEM((buffer_len, LANES), F32),
                pltpu.VMEM((buffer_len, LANES), F32),
                pltpu.VMEM((4 * CHUNK, LANES), F32),
                pltpu.VMEM((4 * CHUNK, LANES), F32),
                pltpu.SemaphoreType.DMA,
            ],
            compiler_params=pltpu.CompilerParams(vmem_limit_bytes=22 * 1024 * 1024),
            cost_estimate=pl.CostEstimate(flops=2 * 10**9, bytes_accessed=2 * 10**7, transcendentals=0),
            name=f"edge{stage}",
        )(*args)
        edge_lam, edge_u, edge_own = outs[:3]
        arrived = exchange(outs[3:])

        args = [idx_in, flag_in, block_level, geo, lam, edge_lam, edge_own]
        if fwd:
            args += [state, edge_u]
        extra = []
        if stage == 2:
            args += [edge_lam3]
            extra = [lam3]
        if stage == 3:
            extra = [state0, lam4, products]
        plain = len(args) - 3
        args += extra + [lift_back, own_back, trace_back, trace_fwd, all_fwd]
        count = (1, 2, 3, 0)[stage]
        out_shape = (row,) * count
        out_specs = (VMEM,) * count
        scratch = [
            pltpu.VMEM((4 * elements + SPREAD, LANES), F32),
            pltpu.VMEM((4 * elements + SPREAD, LANES), F32),
            pltpu.VMEM((4 * CHUNK, LANES), F32),
            pltpu.VMEM((4 * CHUNK, LANES), F32),
        ]
        if stage == 3:
            scratch = [pltpu.VMEM((elements, LANES), F32)] * 2 + scratch
            out_shape = (shape((width, elements), F32), shape((1, elements), F32), edge_row)
            out_specs = (HBM, VMEM, VMEM)
        if extra:
            scratch += [
                pltpu.VMEM((2, len(extra), CHUNK, LANES), F32),
                pltpu.SemaphoreType.DMA((2, len(extra))),
            ]
        if stage == 3:
            scratch += [
                pltpu.VMEM((elements // CHUNK - 1, width, CHUNK), F32),
                pltpu.SemaphoreType.DMA((elements // CHUNK - 1,)),
            ]
        if stage == 1:
            lam3, edge_lam3 = lam, edge_lam
        outs = pl.pallas_call(
            functools.partial(interior_kernel, stage, elements),
            out_shape=out_shape,
            in_specs=[SMEM] * 3 + [VMEM] * plain + [ANY] * len(extra) + [VMEM] * 5,
            out_specs=out_specs,
            scratch_shapes=scratch,
            compiler_params=pltpu.CompilerParams(vmem_limit_bytes=(27, 28, 29, 41)[stage] * 1024 * 1024),
            cost_estimate=pl.CostEstimate(flops=10**10, bytes_accessed=10**8, transcendentals=0),
            name=f"inner{stage}",
        )(*args)
        if stage == 3:
            adjoint, gradient, first = outs
            break
        lam = outs[0]
        if stage == 2:
            products = outs[1]
        if fwd:
            state = outs[-1]

    adjoint = pl.pallas_call(
        final_kernel,
        out_shape=shape((width, elements), F32),
        in_specs=[HBM] + [VMEM] * 5,
        out_specs=HBM,
        scratch_shapes=[pltpu.VMEM((width, BOUND), F32), pltpu.SemaphoreType.DMA],
        input_output_aliases={0: 0},
        name="final",
    )(adjoint, first, *arrived)
    return adjoint, gradient.reshape(-1)


def solution(mesh):
    in_specs = (
        P(None, ("slab", "dom")),
        P(None, ("slab", "dom")),
        P(("slab", "dom")),
        P(("slab", "dom")),
        P(("slab", "dom")),
        P(None, ("slab", "dom")),
        P(),
        P(),
        P(),
    )
    out_specs = (P(None, ("slab", "dom")), P(("slab", "dom")))
    return jax.shard_map(local, mesh=mesh, in_specs=in_specs, out_specs=out_specs, check_vma=False)
```

```python
import functools

import jax
import jax.numpy as jnp
from jax import lax
from jax.experimental import pallas as pl
from jax.experimental.pallas import tpu as pltpu
from jax.sharding import PartitionSpec as P

BLK = 256
BOUND = 1024
CHUNK = BOUND
PER = CHUNK // BLK
LANES = 128
HALF = 64
UNROLL = BLK
LINE = 128
SPREAD = 64
F32 = jnp.float32
BF16 = jnp.bfloat16

base_step = 0.05
lowest_level = (2, 1, 2, 0)

SMEM = pl.BlockSpec(memory_space=pltpu.SMEM)
VMEM = pl.BlockSpec(memory_space=pltpu.VMEM)
ANY = pl.BlockSpec(memory_space=pl.ANY)
HBM = pl.BlockSpec(memory_space=pltpu.HBM)


def mm(a, b, dims=((1,), (0,))):
    return lax.dot_general(a, b, (dims, ((), ())), preferred_element_type=F32)


def block_step(level, lowest):
    size = jnp.where(
        level == 2, base_step, jnp.where(level == 1, 2.0 * base_step, 4.0 * base_step)
    )
    return jnp.where(level >= lowest, size, 0.0).astype(F32)


def chunk_step(level_ref, c, lowest):
    parts = [
        jnp.full((BLK, LANES), block_step(level_ref[c * PER + i], lowest), F32) for i in range(PER)
    ]
    return jnp.concatenate(parts, axis=0)


def active_blocks(level_ref, blocks, lowest):
    count = jnp.int32(0)
    for b in range(blocks):
        count = count + jnp.where(level_ref[b] >= lowest, 1, 0)
    return count


def rows_of(c):
    return pl.ds(pl.multiple_of(c * CHUNK, CHUNK), CHUNK)


def move_rows(idx_ref, flag_ref, c, count, source, accs, p_ref, g_ref):
    lines = idx_ref.shape[0] // 4

    def group(q, _):
        face = q & 3
        block = q >> 2
        line = face * lines + c * (CHUNK // LINE) + block * (BLK // LINE)
        pos = pl.multiple_of(face * CHUNK + block * BLK, BLK)

        def fast():
            for t in range(UNROLL // 4):
                acc = accs[t % 2]
                ii = [idx_ref[line + 4 * t // LINE, 4 * t % LINE + r] for r in range(4)]
                vals = [acc[pl.ds(i, 1), :] for i in ii]
                if g_ref is not None:
                    for r in range(4):
                        got = vals[r] if source is None else source[pl.ds(ii[r], 1), :]
                        g_ref[pl.ds(pos + 4 * t + r, 1), :] = got
                for r in range(4):
                    acc[pl.ds(ii[r], 1), :] = vals[r] + p_ref[pl.ds(pos + 4 * t + r, 1), :]

        def slow():
            def some(n, _):
                first = n * 16
                at = line + (n >> 3)
                for r in range(16):
                    acc = accs[r % 2]
                    i = idx_ref[at, (first & (LINE - 1)) + r]
                    val = acc[pl.ds(i, 1), :]
                    if g_ref is not None:
                        got = val if source is None else source[pl.ds(i, 1), :]
                        g_ref[pl.ds(pos + first + r, 1), :] = got
                    acc[pl.ds(i, 1), :] = val + p_ref[pl.ds(pos + first + r, 1), :]
                return 0

            lax.fori_loop(0, UNROLL // 16, some, 0)

        clash = flag_ref[face, c * PER + block]
        pl.when(clash == 0)(fast)
        pl.when(clash != 0)(slow)
        return 0

    lax.fori_loop(0, count * 4, group, 0)


def setup_kernel(
    link_ref, jac_ref, cond_ref, stiff_ref, lift_ref, trace_ref,
    row_out, slot_out, flag_in, flag_edge, small_out,
    trace_fwd, trace_back, lift_back, own_back, all_fwd,
    edge_back, edge_fwd, dup_ref,
):
    face_rows, width = lift_ref.shape
    nodes = face_rows // 4
    elements = link_ref.shape[1]

    code = link_ref[...]
    face = code % 4
    slot = code // 4
    place = lax.broadcasted_iota(jnp.int32, code.shape, 1)
    row = jnp.where(slot < elements, face * elements + slot, 4 * elements + place % SPREAD)
    for table, out in ((row, row_out), (slot, slot_out)):
        lines = out.shape[0] // 4
        for g in range(lines):
            out[pl.ds(g, 4, stride=lines), :] = table[:, g * LINE : (g + 1) * LINE]
    small_out[...] = jnp.zeros_like(small_out)
    small_out[0:1, :] = jac_ref[...]
    small_out[1:2, :] = cond_ref[...]
    small_out[2:6, :] = face.astype(F32)

    def flags(table, out):
        count = table.shape[1]
        at = lax.broadcasted_iota(jnp.int32, table.shape, 1)
        dup = jnp.zeros(table.shape, F32)
        for d in range(1, 4):
            moved = pltpu.roll(table, d, 1)
            dup = jnp.where((table == moved) & (at % 4 >= d), 1.0, dup)
        dup_ref[...] = jnp.zeros_like(dup_ref)
        dup_ref[0:4, 0:count] = dup
        first = lax.broadcasted_iota(jnp.int32, (count, LANES), 0) // UNROLL
        second = lax.broadcasted_iota(jnp.int32, (count, LANES), 1)
        pick = jnp.where(first == second, 1.0, 0.0).astype(BF16)
        total = mm(dup_ref[:, 0:count].astype(BF16), pick)
        out[...] = total.astype(jnp.int32)

    flags(row, flag_in)
    flags(slot[:, :BOUND], flag_edge)

    def pick(rows, columns, lane, group, face_of):
        r = lax.broadcasted_iota(jnp.int32, (rows, columns), 0)
        c = lax.broadcasted_iota(jnp.int32, (rows, columns), 1)
        q = c % group - lane
        hit = (r == 4 * q + face_of(c // group)) & (q >= 0) & (q < nodes)
        return jnp.where(hit, 1.0, 0.0).astype(BF16)

    def put(ref, value, at=None):
        value = value.astype(BF16)
        rows, columns = value.shape
        if at is None:
            ref[...] = jnp.zeros_like(ref)
            at = 0
        ref[at : at + rows, 0:columns] = value

    lift = lift_ref[...]
    trace = trace_ref[...]
    stiff = stiff_ref[...]
    low = pick(face_rows, 4 * LANES, 0, LANES, lambda g: g)
    high = pick(face_rows, 4 * LANES, HALF, LANES, lambda g: g)
    put(trace_fwd, mm(trace, low, ((0,), (0,))))
    put(trace_back, mm(high, trace, ((0,), (0,))))
    put(lift_back, mm(lift, high, ((0,), (0,))))
    put(all_fwd, mm(low, lift, ((0,), (0,))))
    edge_back[...] = jnp.zeros_like(edge_back)
    edge_fwd[...] = jnp.zeros_like(edge_fwd)
    one_face = [pick(face_rows, HALF, 0, HALF, lambda g, j=j: j) for j in range(4)]
    lifts = [mm(lift, one_face[j], ((0,), (0,))).astype(BF16) for j in range(4)]
    traces = [mm(one_face[k], trace, ((0,), (0,))).astype(BF16) for k in range(4)]
    for j in range(4):
        for k in range(4):
            at = k * LANES
            edge_back[j, 0:width, at : at + width] = mm(lifts[j], traces[k]).astype(BF16)
            put(edge_fwd, mm(traces[k], lifts[j], ((0,), (1,))), 4 * j * LANES + at)
    own = stiff.astype(F32) - mm(lift, trace, ((0,), (0,)))
    r = lax.broadcasted_iota(jnp.int32, (width, width), 0)
    c = lax.broadcasted_iota(jnp.int32, (width, width), 1)
    unit = jnp.where(r == c, 1.0, 0.0).astype(BF16)
    turned = mm(unit, stiff, ((1,), (1,))) - mm(trace, lift, ((0,), (0,)))
    put(own_back, own)
    put(own_back, own - own.astype(BF16).astype(F32), LANES)
    for ref, at in ((all_fwd, 4 * LANES), (edge_fwd, 16 * LANES)):
        put(ref, turned, at)
        put(ref, turned - turned.astype(BF16).astype(F32), at + LANES)


def prep_kernel(x_ref, c_ref, s_ref, u_out, lam_out, geo_out, buf):
    width, elements = x_ref.shape
    buf[...] = jnp.zeros_like(buf)

    def turn(c, _):
        at = pl.ds(pl.multiple_of(c * CHUNK, CHUNK), CHUNK)
        buf[:width, :] = x_ref[:, at]
        u_out[at, :] = buf[...].T
        buf[:width, :] = c_ref[:, at]
        lam_out[at, :] = buf[...].T
        geo_out[at, :] = jnp.concatenate(
            [s_ref[:, at].T, jnp.zeros((CHUNK, LANES - s_ref.shape[0]), F32)], axis=1
        )
        return 0

    lax.fori_loop(0, elements // CHUNK, turn, 0)


def boundary_kernel(stage, elements, *refs):
    fwd = stage > 0
    lowest = lowest_level[3 - stage]
    refs = list(refs)
    idx_ref, flag_ref, level_ref, side_ref, geo_ref, u_ref, lam_ref = refs[:7]
    del refs[:7]
    arrived = []
    if fwd:
        arrived = refs[:4]
        del refs[:4]
    back_ops, fwd_ops = refs[:2]
    lam_out, u_out, own_out = refs[2:5]
    sends = refs[5:9]
    ubuf, acc0, acc1, p_ref, g_ref, sem = refs[9:]
    active = jnp.minimum(active_blocks(level_ref, PER, lowest), PER)
    up_slab, up_dom = side_ref[0], side_ref[1]
    regions = (up_slab, 1 - up_slab, 2 + up_dom, 3 - up_dom)

    def region(r):
        return pl.ds(pl.multiple_of(elements + regions[r] * BOUND, BOUND), BOUND)

    if fwd:
        copy = pltpu.make_async_copy(u_ref, ubuf.at[pl.ds(0, elements)], sem)
        copy.start()
        for r in range(4):
            ubuf[region(r), :] = arrived[r][1].astype(F32)
        g_ref[...] = jnp.zeros_like(g_ref)
    acc0[...] = jnp.zeros_like(acc0)
    acc1[...] = jnp.zeros_like(acc1)

    lam = lam_ref[0:BOUND, :]
    for a in arrived:
        lam = lam + a[0].astype(F32)
    lam_out[...] = lam
    geo = geo_ref[0:BOUND, :]
    weighted = (geo[:, 0:1] * (chunk_step(level_ref, 0, lowest) * lam)).astype(BF16)
    for j in range(4):
        for n in range(0, BOUND, BLK):
            face = jnp.broadcast_to(geo_ref[n : n + BLK, 2 + j : 3 + j], (BLK, LANES))
            every = mm(weighted[n : n + BLK, :], back_ops[j])
            part = every[:, 0:LANES]
            for k in range(1, 4):
                part = jnp.where(face == k, every[:, k * LANES : (k + 1) * LANES], part)
            p_ref[j * BOUND + n : j * BOUND + n + BLK, :] = part
    if fwd:
        copy.wait()
    move_rows(idx_ref, flag_ref, 0, active, ubuf, (acc0, acc1), p_ref, g_ref if fwd else None)
    if not fwd:
        u_out[...] = u_ref[0:BOUND, :]
    for n in range(0, BOUND if fwd else 0, BLK):
        at = slice(n, n + BLK)
        u = u_ref[at, :]
        low = u.astype(BF16)
        parts = []
        for j in range(4):
            face = jnp.broadcast_to(geo_ref[at, 2 + j : 3 + j], (BLK, LANES))
            got = g_ref[j * BOUND + n : j * BOUND + n + BLK, :]
            parts += [jnp.where(face == k, got, 0.0).astype(BF16) for k in range(4)]
        change = mm(jnp.concatenate(parts + [low, low], axis=1), fwd_ops[...])
        geo = geo_ref[at, :]
        step = block_step(level_ref[n // BLK], lowest)
        u_out[at, :] = u + step * (geo[:, 0:1] * change - geo[:, 1:2] * u)
    for r in range(4):
        sends[r][0] = (acc0[region(r), :] + acc1[region(r), :]).astype(BF16)
        if stage < 3:
            sends[r][1] = u_out[...].astype(BF16)

    def total(c, _):
        own_out[rows_of(c), :] = acc0[rows_of(c), :] + acc1[rows_of(c), :]
        return 0

    lax.fori_loop(0, elements // CHUNK, total, 0)


def interior_kernel(stage, elements, *refs):
    fwd = stage > 0
    lowest = lowest_level[3 - stage]
    refs = list(refs)
    idx_ref, flag_ref, level_ref, geo_ref, lam_ref, edge_lam, edge_own = refs[:7]
    del refs[:7]
    if fwd:
        u_ref, edge_u = refs[:2]
        del refs[:2]
    extra = []
    if stage == 2:
        edge_lam3 = refs.pop(0)
        extra = [refs.pop(0)]
    if stage == 3:
        extra = refs[:3]
        del refs[:3]
    lift_back, own_back, trace_back, trace_fwd, all_fwd = refs[:5]
    del refs[:5]
    if stage == 3:
        adj_out, grad_out, first_out = refs[:3]
        del refs[:3]
        turned, turn_sems = refs[-2:]
        del refs[-2:]
    lam_out = refs.pop(0)
    if stage == 2:
        q_out = refs.pop(0)
    if fwd:
        u_out = refs.pop(0)
    tab0, tab1, p_ref, g_ref = refs[:4]
    if extra:
        held, sems = refs[4:]
    chunks = elements // CHUNK
    active = active_blocks(level_ref, level_ref.shape[0], lowest)
    busy_chunks = (active + (PER - 1)) // PER

    def plane(c, k):
        return pl.ds(pl.multiple_of(k * elements + c * CHUNK, CHUNK), CHUNK)

    def fetch(c):
        return [
            pltpu.make_async_copy(ref.at[pl.ds(c * CHUNK, CHUNK)], held.at[c % 2, i], sems.at[c % 2, i])
            for i, ref in enumerate(extra)
        ]

    for copy in fetch(0):
        copy.start()

    def start(c, _):
        if fwd:
            traces = mm(u_ref[rows_of(c), :].astype(BF16), trace_fwd[...])
            traces = traces.astype(BF16).astype(F32)
        for k in range(4):
            part = traces[:, k * LANES : (k + 1) * LANES] if fwd else jnp.zeros((CHUNK, LANES), F32)
            tab0[plane(c, k), :] = part
            tab1[plane(c, k), :] = part
        return 0

    lax.fori_loop(0, chunks, start, 0, unroll=True)
    if fwd:
        g_ref[...] = jnp.zeros_like(g_ref)

    def adjoint(c, lam, links):
        geo = geo_ref[rows_of(c), :]
        scaled = chunk_step(level_ref, c, lowest) * lam
        weighted = (geo[:, 0:1] * scaled).astype(BF16)
        if links:
            lifted = mm(weighted, lift_back[...])
            for j in range(4):
                p_ref[j * CHUNK : (j + 1) * CHUNK, :] = lifted[:, j * LANES : (j + 1) * LANES]
        own = mm(jnp.concatenate([weighted, weighted], axis=1), own_back[...])
        lam_out[rows_of(c), :] = lam - geo[:, 1:2] * scaled + own

    tabs = (tab0, tab1)
    adjoint(0, edge_lam[...], False)
    if fwd:
        u_out[0:CHUNK, :] = edge_u[...]

    def busy(c, _):
        adjoint(c, lam_ref[rows_of(c), :], True)
        count = jnp.minimum(active - c * PER, PER)
        move_rows(idx_ref, flag_ref, c, count, None, tabs, p_ref, g_ref if fwd else None)
        if fwd:
            geo = geo_ref[rows_of(c), :]
            u = u_ref[rows_of(c), :]
            low = u.astype(BF16)
            parts = [g_ref[j * CHUNK : (j + 1) * CHUNK, :].astype(BF16) for j in range(4)]
            change = mm(jnp.concatenate(parts + [low, low], axis=1), all_fwd[...])
            step = chunk_step(level_ref, c, lowest)
            u_out[rows_of(c), :] = u + step * (geo[:, 0:1] * change - geo[:, 1:2] * u)
        return 0

    def idle(c, _):
        lam_out[rows_of(c), :] = lam_ref[rows_of(c), :]
        if fwd:
            u_out[rows_of(c), :] = u_ref[rows_of(c), :]
        return 0

    lax.fori_loop(1, busy_chunks, busy, 0)
    lax.fori_loop(busy_chunks, chunks, idle, 0)

    def collect(c):
        parts = [
            (tab0[plane(c, k), :] + tab1[plane(c, k), :]).astype(BF16) for k in range(4)
        ]
        back = mm(jnp.concatenate(parts, axis=1), trace_back[...])
        at = rows_of(c)
        lam_out[at, :] = lam_out[at, :] + edge_own[at, :] + back

    def multiply(c):
        at = rows_of(c)
        lam = edge_lam[...] if c == 0 else lam_ref[at, :]

        def step(s):
            return chunk_step(level_ref, c, lowest_level[s])

        if stage == 2:
            lam3 = edge_lam3[...] if c == 0 else held[c % 2, 0]
            q_out[at, :] = (step(1) * lam) * u_ref[at, :] + (step(2) * lam3) * u_out[at, :]
        else:
            u0, lam4, before = (held[c % 2, i] for i in range(3))
            total = before + (step(0) * lam) * u0 + (step(3) * lam4) * u_out[at, :]
            where = slice(c * CHUNK, (c + 1) * CHUNK)
            grad_out[0:1, where] = -jnp.sum(total.T, axis=0, keepdims=True)
            if c > 0:
                turned[c - 1] = lam_out[at, :].T[: adj_out.shape[0], :]
                store(c).start()
            else:
                first_out[...] = lam_out[at, :]

    def store(c):
        return pltpu.make_async_copy(
            turned.at[c - 1], adj_out.at[:, pl.ds(c * CHUNK, CHUNK)], turn_sems.at[c - 1]
        )

    if not extra:
        for c in range(chunks):
            collect(c)
        return
    for c in range(chunks):
        if c + 1 < chunks:
            for copy in fetch(c + 1):
                copy.start()
        collect(c)
        for copy in fetch(c):
            copy.wait()
        multiply(c)
    if stage == 3:
        for c in range(1, chunks):
            store(c).wait()


def final_kernel(adj_in, first_ref, *refs):
    arrived = refs[:4]
    adj_out, turned, sem = refs[4:]
    del adj_in
    total = first_ref[...]
    for a in arrived:
        total = total + a[0].astype(F32)
    turned[...] = total.T[: turned.shape[0], :]
    store = pltpu.make_async_copy(turned, adj_out.at[:, pl.ds(0, BOUND)], sem)
    store.start()
    store.wait()


def exchange(parts):
    out = []
    for part, axis, odd in zip(parts, ("slab", "slab", "dom", "dom"), (0, 1, 0, 1), strict=True):
        pairs = []
        for i in range(odd, lax.axis_size(axis) - 1, 2):
            pairs += [(i, i + 1), (i + 1, i)]
        out.append(lax.ppermute(part, axis, pairs))
    return out


def local(
    initial_field, cotangent, jacobian, conductivity, block_level, face_link, stiff, lift, trace_op
):
    width, elements = initial_field.shape
    shape = jax.ShapeDtypeStruct
    square = shape((LANES, 4 * LANES), BF16)
    row = shape((elements, LANES), F32)
    edge_row = shape((BOUND, LANES), F32)

    (
        idx_in, slots, flag_in, flag_edge, small,
        trace_fwd, trace_back, lift_back, own_back, all_fwd, edge_back, edge_fwd,
    ) = pl.pallas_call(
        setup_kernel,
        out_shape=(
            shape((4 * elements // LINE, LINE), jnp.int32),
            shape((4 * BOUND // LINE, LINE), jnp.int32),
            shape((8, LANES), jnp.int32),
            shape((8, LANES), jnp.int32),
            shape((8, elements), F32),
            square,
            shape((4 * LANES, LANES), BF16),
            square,
            shape((2 * LANES, LANES), BF16),
            shape((6 * LANES, LANES), BF16),
            shape((4, LANES, 4 * LANES), BF16),
            shape((18 * LANES, LANES), BF16),
        ),
        in_specs=[VMEM] * 6,
        out_specs=(VMEM,) * 12,
        scratch_shapes=[pltpu.VMEM((8, elements), F32)],
        name="setup",
    )(face_link, jacobian.reshape(1, -1), conductivity.reshape(1, -1), stiff, lift.T, trace_op)
    state, lam, geo = pl.pallas_call(
        prep_kernel,
        out_shape=(row, row, row),
        in_specs=[VMEM] * 3,
        out_specs=(VMEM,) * 3,
        scratch_shapes=[pltpu.VMEM((LANES, CHUNK), F32)],
        compiler_params=pltpu.CompilerParams(vmem_limit_bytes=16 * 1024 * 1024),
        name="prep",
    )(initial_field, cotangent, small)
    side = jnp.stack([1 - lax.axis_index("slab") % 2, 1 - lax.axis_index("dom") % 2]).astype(jnp.int32)

    buffer_len = elements + 4 * BOUND
    arrived = []
    state0, lam4 = state, lam
    for stage in range(4):
        fwd = stage > 0
        args = [slots, flag_edge, block_level, side, geo, state, lam, *arrived, edge_back, edge_fwd]
        payload = shape((2 if stage < 3 else 1, BOUND, LANES), BF16)
        outs = pl.pallas_call(
            functools.partial(boundary_kernel, stage, elements),
            out_shape=(edge_row, edge_row, row) + (payload,) * 4,
            in_specs=[SMEM] * 4 + [VMEM] * (len(args) - 4),
            out_specs=(VMEM,) * 7,
            scratch_shapes=[
                pltpu.VMEM((buffer_len, LANES), F32),
                pltpu.VMEM((buffer_len, LANES), F32),
                pltpu.VMEM((buffer_len, LANES), F32),
                pltpu.VMEM((4 * CHUNK, LANES), F32),
                pltpu.VMEM((4 * CHUNK, LANES), F32),
                pltpu.SemaphoreType.DMA,
            ],
            compiler_params=pltpu.CompilerParams(vmem_limit_bytes=22 * 1024 * 1024),
            cost_estimate=pl.CostEstimate(flops=2 * 10**9, bytes_accessed=2 * 10**7, transcendentals=0),
            name=f"edge{stage}",
        )(*args)
        edge_lam, edge_u, edge_own = outs[:3]
        arrived = exchange(outs[3:])

        args = [idx_in, flag_in, block_level, geo, lam, edge_lam, edge_own]
        if fwd:
            args += [state, edge_u]
        extra = []
        if stage == 2:
            args += [edge_lam3]
            extra = [lam3]
        if stage == 3:
            extra = [state0, lam4, products]
        plain = len(args) - 3
        args += extra + [lift_back, own_back, trace_back, trace_fwd, all_fwd]
        count = (1, 2, 3, 0)[stage]
        out_shape = (row,) * count
        out_specs = (VMEM,) * count
        scratch = [
            pltpu.VMEM((4 * elements + SPREAD, LANES), F32),
            pltpu.VMEM((4 * elements + SPREAD, LANES), F32),
            pltpu.VMEM((4 * CHUNK, LANES), F32),
            pltpu.VMEM((4 * CHUNK, LANES), F32),
        ]
        if stage == 3:
            scratch = [pltpu.VMEM((elements, LANES), F32)] * 2 + scratch
            out_shape = (shape((width, elements), F32), shape((1, elements), F32), edge_row)
            out_specs = (HBM, VMEM, VMEM)
        if extra:
            scratch += [
                pltpu.VMEM((2, len(extra), CHUNK, LANES), F32),
                pltpu.SemaphoreType.DMA((2, len(extra))),
            ]
        if stage == 3:
            scratch += [
                pltpu.VMEM((elements // CHUNK - 1, width, CHUNK), F32),
                pltpu.SemaphoreType.DMA((elements // CHUNK - 1,)),
            ]
        if stage == 1:
            lam3, edge_lam3 = lam, edge_lam
        outs = pl.pallas_call(
            functools.partial(interior_kernel, stage, elements),
            out_shape=out_shape,
            in_specs=[SMEM] * 3 + [VMEM] * plain + [ANY] * len(extra) + [VMEM] * 5,
            out_specs=out_specs,
            scratch_shapes=scratch,
            compiler_params=pltpu.CompilerParams(vmem_limit_bytes=(27, 28, 29, 41)[stage] * 1024 * 1024),
            cost_estimate=pl.CostEstimate(flops=10**10, bytes_accessed=10**8, transcendentals=0),
            name=f"inner{stage}",
        )(*args)
        if stage == 3:
            adjoint, gradient, first = outs
            break
        lam = outs[0]
        if stage == 2:
            products = outs[1]
        if fwd:
            state = outs[-1]

    adjoint = pl.pallas_call(
        final_kernel,
        out_shape=shape((width, elements), F32),
        in_specs=[HBM] + [VMEM] * 5,
        out_specs=HBM,
        scratch_shapes=[pltpu.VMEM((width, BOUND), F32), pltpu.SemaphoreType.DMA],
        input_output_aliases={0: 0},
        name="final",
    )(adjoint, first, *arrived)
    return adjoint, gradient.reshape(-1)


def solution(mesh):
    in_specs = (
        P(None, ("slab", "dom")),
        P(None, ("slab", "dom")),
        P(("slab", "dom")),
        P(("slab", "dom")),
        P(("slab", "dom")),
        P(None, ("slab", "dom")),
        P(),
        P(),
        P(),
    )
    out_specs = (P(None, ("slab", "dom")), P(("slab", "dom")))
    return jax.shard_map(local, mesh=mesh, in_specs=in_specs, out_specs=out_specs, check_vma=False)
```

```python
import functools

import jax
import jax.numpy as jnp
from jax import lax
from jax.experimental import pallas as pl
from jax.experimental.pallas import tpu as pltpu
from jax.sharding import PartitionSpec as P

BLK = 256
BOUND = 1024
CHUNK = BOUND
PER = CHUNK // BLK
LANES = 128
HALF = 64
UNROLL = BLK
LINE = 128
SPREAD = 64
F32 = jnp.float32
BF16 = jnp.bfloat16

base_step = 0.05
lowest_level = (2, 1, 2, 0)

SMEM = pl.BlockSpec(memory_space=pltpu.SMEM)
VMEM = pl.BlockSpec(memory_space=pltpu.VMEM)
ANY = pl.BlockSpec(memory_space=pl.ANY)
HBM = pl.BlockSpec(memory_space=pltpu.HBM)


def mm(a, b, dims=((1,), (0,))):
    return lax.dot_general(a, b, (dims, ((), ())), preferred_element_type=F32)


def block_step(level, lowest):
    size = jnp.where(
        level == 2, base_step, jnp.where(level == 1, 2.0 * base_step, 4.0 * base_step)
    )
    return jnp.where(level >= lowest, size, 0.0).astype(F32)


def chunk_step(level_ref, c, lowest):
    parts = [
        jnp.full((BLK, LANES), block_step(level_ref[c * PER + i], lowest), F32) for i in range(PER)
    ]
    return jnp.concatenate(parts, axis=0)


def active_blocks(level_ref, blocks, lowest):
    count = jnp.int32(0)
    for b in range(blocks):
        count = count + jnp.where(level_ref[b] >= lowest, 1, 0)
    return count


def rows_of(c):
    return pl.ds(pl.multiple_of(c * CHUNK, CHUNK), CHUNK)


def move_rows(idx_ref, flag_ref, c, count, source, accs, p_ref, g_ref):
    lines = idx_ref.shape[0] // 4

    def group(q, _):
        face = q & 3
        block = q >> 2
        line = face * lines + c * (CHUNK // LINE) + block * (BLK // LINE)
        pos = pl.multiple_of(face * CHUNK + block * BLK, BLK)

        def fast():
            for t in range(UNROLL // 4):
                acc = accs[t % 2]
                ii = [idx_ref[line + 4 * t // LINE, 4 * t % LINE + r] for r in range(4)]
                vals = [acc[pl.ds(i, 1), :] for i in ii]
                if g_ref is not None:
                    for r in range(4):
                        got = vals[r] if source is None else source[pl.ds(ii[r], 1), :]
                        g_ref[pl.ds(pos + 4 * t + r, 1), :] = got
                for r in range(4):
                    acc[pl.ds(ii[r], 1), :] = vals[r] + p_ref[pl.ds(pos + 4 * t + r, 1), :]

        def slow():
            def some(n, _):
                first = n * 16
                at = line + (n >> 3)
                for r in range(16):
                    acc = accs[r % 2]
                    i = idx_ref[at, (first & (LINE - 1)) + r]
                    val = acc[pl.ds(i, 1), :]
                    if g_ref is not None:
                        got = val if source is None else source[pl.ds(i, 1), :]
                        g_ref[pl.ds(pos + first + r, 1), :] = got
                    acc[pl.ds(i, 1), :] = val + p_ref[pl.ds(pos + first + r, 1), :]
                return 0

            lax.fori_loop(0, UNROLL // 16, some, 0)

        clash = flag_ref[face, c * PER + block]
        pl.when(clash == 0)(fast)
        pl.when(clash != 0)(slow)
        return 0

    lax.fori_loop(0, count * 4, group, 0)


def setup_kernel(
    link_ref, jac_ref, cond_ref, stiff_ref, lift_ref, trace_ref,
    row_out, slot_out, flag_in, flag_edge, small_out,
    trace_fwd, trace_back, lift_back, own_back, all_fwd,
    edge_back, edge_fwd, dup_ref,
):
    face_rows, width = lift_ref.shape
    nodes = face_rows // 4
    elements = link_ref.shape[1]

    code = link_ref[...]
    face = code % 4
    slot = code // 4
    place = lax.broadcasted_iota(jnp.int32, code.shape, 1)
    row = jnp.where(slot < elements, face * elements + slot, 4 * elements + place % SPREAD)
    for table, out in ((row, row_out), (slot, slot_out)):
        lines = out.shape[0] // 4
        for g in range(lines):
            out[pl.ds(g, 4, stride=lines), :] = table[:, g * LINE : (g + 1) * LINE]
    small_out[...] = jnp.zeros_like(small_out)
    small_out[0:1, :] = jac_ref[...]
    small_out[1:2, :] = cond_ref[...]
    small_out[2:6, :] = face.astype(F32)

    def flags(table, out):
        count = table.shape[1]
        at = lax.broadcasted_iota(jnp.int32, table.shape, 1)
        dup = jnp.zeros(table.shape, F32)
        for d in range(1, 4):
            moved = pltpu.roll(table, d, 1)
            dup = jnp.where((table == moved) & (at % 4 >= d), 1.0, dup)
        dup_ref[...] = jnp.zeros_like(dup_ref)
        dup_ref[0:4, 0:count] = dup
        first = lax.broadcasted_iota(jnp.int32, (count, LANES), 0) // UNROLL
        second = lax.broadcasted_iota(jnp.int32, (count, LANES), 1)
        pick = jnp.where(first == second, 1.0, 0.0).astype(BF16)
        total = mm(dup_ref[:, 0:count].astype(BF16), pick)
        out[...] = total.astype(jnp.int32)

    flags(row, flag_in)
    flags(slot[:, :BOUND], flag_edge)

    def pick(rows, columns, lane, group, face_of):
        r = lax.broadcasted_iota(jnp.int32, (rows, columns), 0)
        c = lax.broadcasted_iota(jnp.int32, (rows, columns), 1)
        q = c % group - lane
        hit = (r == 4 * q + face_of(c // group)) & (q >= 0) & (q < nodes)
        return jnp.where(hit, 1.0, 0.0).astype(BF16)

    def put(ref, value, at=None):
        value = value.astype(BF16)
        rows, columns = value.shape
        if at is None:
            ref[...] = jnp.zeros_like(ref)
            at = 0
        ref[at : at + rows, 0:columns] = value

    lift = lift_ref[...]
    trace = trace_ref[...]
    stiff = stiff_ref[...]
    low = pick(face_rows, 4 * LANES, 0, LANES, lambda g: g)
    high = pick(face_rows, 4 * LANES, HALF, LANES, lambda g: g)
    put(trace_fwd, mm(trace, low, ((0,), (0,))))
    put(trace_back, mm(high, trace, ((0,), (0,))))
    put(lift_back, mm(lift, high, ((0,), (0,))))
    put(all_fwd, mm(low, lift, ((0,), (0,))))
    edge_back[...] = jnp.zeros_like(edge_back)
    edge_fwd[...] = jnp.zeros_like(edge_fwd)
    one_face = [pick(face_rows, HALF, 0, HALF, lambda g, j=j: j) for j in range(4)]
    lifts = [mm(lift, one_face[j], ((0,), (0,))).astype(BF16) for j in range(4)]
    traces = [mm(one_face[k], trace, ((0,), (0,))).astype(BF16) for k in range(4)]
    for j in range(4):
        for k in range(4):
            at = k * LANES
            edge_back[j, 0:width, at : at + width] = mm(lifts[j], traces[k]).astype(BF16)
            put(edge_fwd, mm(traces[k], lifts[j], ((0,), (1,))), 4 * j * LANES + at)
    own = stiff.astype(F32) - mm(lift, trace, ((0,), (0,)))
    r = lax.broadcasted_iota(jnp.int32, (width, width), 0)
    c = lax.broadcasted_iota(jnp.int32, (width, width), 1)
    unit = jnp.where(r == c, 1.0, 0.0).astype(BF16)
    turned = mm(unit, stiff, ((1,), (1,))) - mm(trace, lift, ((0,), (0,)))
    put(own_back, own)
    put(own_back, own - own.astype(BF16).astype(F32), LANES)
    for ref, at in ((all_fwd, 4 * LANES), (edge_fwd, 16 * LANES)):
        put(ref, turned, at)
        put(ref, turned - turned.astype(BF16).astype(F32), at + LANES)


def prep_kernel(x_ref, c_ref, s_ref, u_out, lam_out, geo_out, buf):
    width, elements = x_ref.shape
    buf[...] = jnp.zeros_like(buf)

    def turn(c, _):
        at = pl.ds(pl.multiple_of(c * CHUNK, CHUNK), CHUNK)
        buf[:width, :] = x_ref[:, at]
        u_out[at, :] = buf[...].T
        buf[:width, :] = c_ref[:, at]
        lam_out[at, :] = buf[...].T
        geo_out[at, :] = jnp.concatenate(
            [s_ref[:, at].T, jnp.zeros((CHUNK, LANES - s_ref.shape[0]), F32)], axis=1
        )
        return 0

    lax.fori_loop(0, elements // CHUNK, turn, 0)


def boundary_kernel(stage, elements, *refs):
    fwd = stage > 0
    lowest = lowest_level[3 - stage]
    refs = list(refs)
    idx_ref, flag_ref, level_ref, side_ref, geo_ref, u_ref, lam_ref = refs[:7]
    del refs[:7]
    arrived = []
    if fwd:
        arrived = refs[:4]
        del refs[:4]
    back_ops, fwd_ops = refs[:2]
    lam_out, u_out, own_out = refs[2:5]
    sends = refs[5:9]
    ubuf, acc0, acc1, p_ref, g_ref, sem = refs[9:]
    active = jnp.minimum(active_blocks(level_ref, PER, lowest), PER)
    up_slab, up_dom = side_ref[0], side_ref[1]
    regions = (up_slab, 1 - up_slab, 2 + up_dom, 3 - up_dom)

    def region(r):
        return pl.ds(pl.multiple_of(elements + regions[r] * BOUND, BOUND), BOUND)

    if fwd:
        copy = pltpu.make_async_copy(u_ref, ubuf.at[pl.ds(0, elements)], sem)
        copy.start()
        for r in range(4):
            ubuf[region(r), :] = arrived[r][1].astype(F32)
        g_ref[...] = jnp.zeros_like(g_ref)
    acc0[...] = jnp.zeros_like(acc0)
    acc1[...] = jnp.zeros_like(acc1)

    lam = lam_ref[0:BOUND, :]
    for a in arrived:
        lam = lam + a[0].astype(F32)
    lam_out[...] = lam
    geo = geo_ref[0:BOUND, :]
    weighted = (geo[:, 0:1] * (chunk_step(level_ref, 0, lowest) * lam)).astype(BF16)
    for j in range(4):
        for n in range(0, BOUND, BLK):
            face = jnp.broadcast_to(geo_ref[n : n + BLK, 2 + j : 3 + j], (BLK, LANES))
            every = mm(weighted[n : n + BLK, :], back_ops[j])
            part = every[:, 0:LANES]
            for k in range(1, 4):
                part = jnp.where(face == k, every[:, k * LANES : (k + 1) * LANES], part)
            p_ref[j * BOUND + n : j * BOUND + n + BLK, :] = part
    if fwd:
        copy.wait()
    move_rows(idx_ref, flag_ref, 0, active, ubuf, (acc0, acc1), p_ref, g_ref if fwd else None)
    if not fwd:
        u_out[...] = u_ref[0:BOUND, :]
    for n in range(0, BOUND if fwd else 0, BLK):
        at = slice(n, n + BLK)
        u = u_ref[at, :]
        low = u.astype(BF16)
        parts = []
        for j in range(4):
            face = jnp.broadcast_to(geo_ref[at, 2 + j : 3 + j], (BLK, LANES))
            got = g_ref[j * BOUND + n : j * BOUND + n + BLK, :]
            parts += [jnp.where(face == k, got, 0.0).astype(BF16) for k in range(4)]
        change = mm(jnp.concatenate(parts + [low, low], axis=1), fwd_ops[...])
        geo = geo_ref[at, :]
        step = block_step(level_ref[n // BLK], lowest)
        u_out[at, :] = u + step * (geo[:, 0:1] * change - geo[:, 1:2] * u)
    for r in range(4):
        sends[r][0] = (acc0[region(r), :] + acc1[region(r), :]).astype(BF16)
        if stage < 3:
            sends[r][1] = u_out[...].astype(BF16)

    def total(c, _):
        own_out[rows_of(c), :] = acc0[rows_of(c), :] + acc1[rows_of(c), :]
        return 0

    lax.fori_loop(0, elements // CHUNK, total, 0)


def interior_kernel(stage, elements, *refs):
    fwd = stage > 0
    lowest = lowest_level[3 - stage]
    refs = list(refs)
    idx_ref, flag_ref, level_ref, geo_ref, lam_ref, edge_lam, edge_own = refs[:7]
    del refs[:7]
    if fwd:
        u_ref, edge_u = refs[:2]
        del refs[:2]
    extra = []
    if stage == 2:
        edge_lam3 = refs.pop(0)
        extra = [refs.pop(0)]
    if stage == 3:
        extra = refs[:3]
        del refs[:3]
    lift_back, own_back, trace_back, trace_fwd, all_fwd = refs[:5]
    del refs[:5]
    if stage == 3:
        adj_out, grad_out, first_out = refs[:3]
        del refs[:3]
        turned, turn_sems = refs[-2:]
        del refs[-2:]
    lam_out = refs.pop(0)
    if stage == 2:
        q_out = refs.pop(0)
    if fwd:
        u_out = refs.pop(0)
    tab0, tab1, p_ref, g_ref = refs[:4]
    if extra:
        held, sems = refs[4:]
    chunks = elements // CHUNK
    active = active_blocks(level_ref, level_ref.shape[0], lowest)
    busy_chunks = (active + (PER - 1)) // PER

    def plane(c, k):
        return pl.ds(pl.multiple_of(k * elements + c * CHUNK, CHUNK), CHUNK)

    def fetch(c):
        return [
            pltpu.make_async_copy(ref.at[pl.ds(c * CHUNK, CHUNK)], held.at[c % 2, i], sems.at[c % 2, i])
            for i, ref in enumerate(extra)
        ]

    for copy in fetch(0):
        copy.start()

    def start(c, _):
        if fwd:
            traces = mm(u_ref[rows_of(c), :].astype(BF16), trace_fwd[...])
            traces = traces.astype(BF16).astype(F32)
        for k in range(4):
            part = traces[:, k * LANES : (k + 1) * LANES] if fwd else jnp.zeros((CHUNK, LANES), F32)
            tab0[plane(c, k), :] = part
            tab1[plane(c, k), :] = part
        return 0

    lax.fori_loop(0, chunks, start, 0, unroll=True)
    if fwd:
        g_ref[...] = jnp.zeros_like(g_ref)

    def piece(c, n):
        return pl.ds(pl.multiple_of(c * CHUNK + n, BLK), BLK)

    def adjoint(c, lam_in, links):
        for n in range(0, CHUNK, BLK):
            at = piece(c, n)
            lam = lam_in[pl.ds(n, BLK), :] if links is False else lam_in[at, :]
            geo = geo_ref[at, :]
            scaled = block_step(level_ref[c * PER + n // BLK], lowest) * lam
            weighted = (geo[:, 0:1] * scaled).astype(BF16)
            if links:
                lifted = mm(weighted, lift_back[...])
                for j in range(4):
                    p_ref[j * CHUNK + n : j * CHUNK + n + BLK, :] = lifted[:, j * LANES : (j + 1) * LANES]
            own = mm(jnp.concatenate([weighted, weighted], axis=1), own_back[...])
            lam_out[at, :] = lam - geo[:, 1:2] * scaled + own

    tabs = (tab0, tab1)
    adjoint(0, edge_lam, False)
    if fwd:
        u_out[0:CHUNK, :] = edge_u[...]

    def busy(c, _):
        adjoint(c, lam_ref, True)
        count = jnp.minimum(active - c * PER, PER)
        move_rows(idx_ref, flag_ref, c, count, None, tabs, p_ref, g_ref if fwd else None)
        for n in range(0, CHUNK if fwd else 0, BLK):
            at = piece(c, n)
            geo = geo_ref[at, :]
            u = u_ref[at, :]
            low = u.astype(BF16)
            parts = [g_ref[j * CHUNK + n : j * CHUNK + n + BLK, :].astype(BF16) for j in range(4)]
            change = mm(jnp.concatenate(parts + [low, low], axis=1), all_fwd[...])
            step = block_step(level_ref[c * PER + n // BLK], lowest)
            u_out[at, :] = u + step * (geo[:, 0:1] * change - geo[:, 1:2] * u)
        return 0

    def idle(c, _):
        lam_out[rows_of(c), :] = lam_ref[rows_of(c), :]
        if fwd:
            u_out[rows_of(c), :] = u_ref[rows_of(c), :]
        return 0

    lax.fori_loop(1, busy_chunks, busy, 0)
    lax.fori_loop(busy_chunks, chunks, idle, 0)

    def collect(c):
        parts = [
            (tab0[plane(c, k), :] + tab1[plane(c, k), :]).astype(BF16) for k in range(4)
        ]
        back = mm(jnp.concatenate(parts, axis=1), trace_back[...])
        at = rows_of(c)
        lam_out[at, :] = lam_out[at, :] + edge_own[at, :] + back

    def multiply(c):
        at = rows_of(c)
        lam = edge_lam[...] if c == 0 else lam_ref[at, :]

        def step(s):
            return chunk_step(level_ref, c, lowest_level[s])

        if stage == 2:
            lam3 = edge_lam3[...] if c == 0 else held[c % 2, 0]
            q_out[at, :] = (step(1) * lam) * u_ref[at, :] + (step(2) * lam3) * u_out[at, :]
        else:
            u0, lam4, before = (held[c % 2, i] for i in range(3))
            total = before + (step(0) * lam) * u0 + (step(3) * lam4) * u_out[at, :]
            where = slice(c * CHUNK, (c + 1) * CHUNK)
            grad_out[0:1, where] = -jnp.sum(total.T, axis=0, keepdims=True)
            if c > 0:
                turned[c - 1] = lam_out[at, :].T[: adj_out.shape[0], :]
                store(c).start()
            else:
                first_out[...] = lam_out[at, :]

    def store(c):
        return pltpu.make_async_copy(
            turned.at[c - 1], adj_out.at[:, pl.ds(c * CHUNK, CHUNK)], turn_sems.at[c - 1]
        )

    if not extra:
        for c in range(chunks):
            collect(c)
        return
    for c in range(chunks):
        if c + 1 < chunks:
            for copy in fetch(c + 1):
                copy.start()
        collect(c)
        for copy in fetch(c):
            copy.wait()
        multiply(c)
    if stage == 3:
        for c in range(1, chunks):
            store(c).wait()


def final_kernel(adj_in, first_ref, *refs):
    arrived = refs[:4]
    adj_out, turned, sem = refs[4:]
    del adj_in
    total = first_ref[...]
    for a in arrived:
        total = total + a[0].astype(F32)
    turned[...] = total.T[: turned.shape[0], :]
    store = pltpu.make_async_copy(turned, adj_out.at[:, pl.ds(0, BOUND)], sem)
    store.start()
    store.wait()


def exchange(parts):
    out = []
    for part, axis, odd in zip(parts, ("slab", "slab", "dom", "dom"), (0, 1, 0, 1), strict=True):
        pairs = []
        for i in range(odd, lax.axis_size(axis) - 1, 2):
            pairs += [(i, i + 1), (i + 1, i)]
        out.append(lax.ppermute(part, axis, pairs))
    return out


def local(
    initial_field, cotangent, jacobian, conductivity, block_level, face_link, stiff, lift, trace_op
):
    width, elements = initial_field.shape
    shape = jax.ShapeDtypeStruct
    square = shape((LANES, 4 * LANES), BF16)
    row = shape((elements, LANES), F32)
    edge_row = shape((BOUND, LANES), F32)

    (
        idx_in, slots, flag_in, flag_edge, small,
        trace_fwd, trace_back, lift_back, own_back, all_fwd, edge_back, edge_fwd,
    ) = pl.pallas_call(
        setup_kernel,
        out_shape=(
            shape((4 * elements // LINE, LINE), jnp.int32),
            shape((4 * BOUND // LINE, LINE), jnp.int32),
            shape((8, LANES), jnp.int32),
            shape((8, LANES), jnp.int32),
            shape((8, elements), F32),
            square,
            shape((4 * LANES, LANES), BF16),
            square,
            shape((2 * LANES, LANES), BF16),
            shape((6 * LANES, LANES), BF16),
            shape((4, LANES, 4 * LANES), BF16),
            shape((18 * LANES, LANES), BF16),
        ),
        in_specs=[VMEM] * 6,
        out_specs=(VMEM,) * 12,
        scratch_shapes=[pltpu.VMEM((8, elements), F32)],
        name="setup",
    )(face_link, jacobian.reshape(1, -1), conductivity.reshape(1, -1), stiff, lift.T, trace_op)
    state, lam, geo = pl.pallas_call(
        prep_kernel,
        out_shape=(row, row, row),
        in_specs=[VMEM] * 3,
        out_specs=(VMEM,) * 3,
        scratch_shapes=[pltpu.VMEM((LANES, CHUNK), F32)],
        compiler_params=pltpu.CompilerParams(vmem_limit_bytes=16 * 1024 * 1024),
        name="prep",
    )(initial_field, cotangent, small)
    side = jnp.stack([1 - lax.axis_index("slab") % 2, 1 - lax.axis_index("dom") % 2]).astype(jnp.int32)

    buffer_len = elements + 4 * BOUND
    arrived = []
    state0, lam4 = state, lam
    for stage in range(4):
        fwd = stage > 0
        args = [slots, flag_edge, block_level, side, geo, state, lam, *arrived, edge_back, edge_fwd]
        payload = shape((2 if stage < 3 else 1, BOUND, LANES), BF16)
        outs = pl.pallas_call(
            functools.partial(boundary_kernel, stage, elements),
            out_shape=(edge_row, edge_row, row) + (payload,) * 4,
            in_specs=[SMEM] * 4 + [VMEM] * (len(args) - 4),
            out_specs=(VMEM,) * 7,
            scratch_shapes=[
                pltpu.VMEM((buffer_len, LANES), F32),
                pltpu.VMEM((buffer_len, LANES), F32),
                pltpu.VMEM((buffer_len, LANES), F32),
                pltpu.VMEM((4 * CHUNK, LANES), F32),
                pltpu.VMEM((4 * CHUNK, LANES), F32),
                pltpu.SemaphoreType.DMA,
            ],
            compiler_params=pltpu.CompilerParams(vmem_limit_bytes=22 * 1024 * 1024),
            cost_estimate=pl.CostEstimate(flops=2 * 10**9, bytes_accessed=2 * 10**7, transcendentals=0),
            name=f"edge{stage}",
        )(*args)
        edge_lam, edge_u, edge_own = outs[:3]
        arrived = exchange(outs[3:])

        args = [idx_in, flag_in, block_level, geo, lam, edge_lam, edge_own]
        if fwd:
            args += [state, edge_u]
        extra = []
        if stage == 2:
            args += [edge_lam3]
            extra = [lam3]
        if stage == 3:
            extra = [state0, lam4, products]
        plain = len(args) - 3
        args += extra + [lift_back, own_back, trace_back, trace_fwd, all_fwd]
        count = (1, 2, 3, 0)[stage]
        out_shape = (row,) * count
        out_specs = (VMEM,) * count
        scratch = [
            pltpu.VMEM((4 * elements + SPREAD, LANES), F32),
            pltpu.VMEM((4 * elements + SPREAD, LANES), F32),
            pltpu.VMEM((4 * CHUNK, LANES), F32),
            pltpu.VMEM((4 * CHUNK, LANES), F32),
        ]
        if stage == 3:
            scratch = [pltpu.VMEM((elements, LANES), F32)] * 2 + scratch
            out_shape = (shape((width, elements), F32), shape((1, elements), F32), edge_row)
            out_specs = (HBM, VMEM, VMEM)
        if extra:
            scratch += [
                pltpu.VMEM((2, len(extra), CHUNK, LANES), F32),
                pltpu.SemaphoreType.DMA((2, len(extra))),
            ]
        if stage == 3:
            scratch += [
                pltpu.VMEM((elements // CHUNK - 1, width, CHUNK), F32),
                pltpu.SemaphoreType.DMA((elements // CHUNK - 1,)),
            ]
        if stage == 1:
            lam3, edge_lam3 = lam, edge_lam
        outs = pl.pallas_call(
            functools.partial(interior_kernel, stage, elements),
            out_shape=out_shape,
            in_specs=[SMEM] * 3 + [VMEM] * plain + [ANY] * len(extra) + [VMEM] * 5,
            out_specs=out_specs,
            scratch_shapes=scratch,
            compiler_params=pltpu.CompilerParams(vmem_limit_bytes=(27, 28, 29, 41)[stage] * 1024 * 1024),
            cost_estimate=pl.CostEstimate(flops=10**10, bytes_accessed=10**8, transcendentals=0),
            name=f"inner{stage}",
        )(*args)
        if stage == 3:
            adjoint, gradient, first = outs
            break
        lam = outs[0]
        if stage == 2:
            products = outs[1]
        if fwd:
            state = outs[-1]

    adjoint = pl.pallas_call(
        final_kernel,
        out_shape=shape((width, elements), F32),
        in_specs=[HBM] + [VMEM] * 5,
        out_specs=HBM,
        scratch_shapes=[pltpu.VMEM((width, BOUND), F32), pltpu.SemaphoreType.DMA],
        input_output_aliases={0: 0},
        name="final",
    )(adjoint, first, *arrived)
    return adjoint, gradient.reshape(-1)


def solution(mesh):
    in_specs = (
        P(None, ("slab", "dom")),
        P(None, ("slab", "dom")),
        P(("slab", "dom")),
        P(("slab", "dom")),
        P(("slab", "dom")),
        P(None, ("slab", "dom")),
        P(),
        P(),
        P(),
    )
    out_specs = (P(None, ("slab", "dom")), P(("slab", "dom")))
    return jax.shard_map(local, mesh=mesh, in_specs=in_specs, out_specs=out_specs, check_vma=False)
```
